32 devices in a mesh: gx: 2 (over x), gy: 4 (over y, core), gz: 4 (over z).
Axes of the slice: x: 2, y: 2, z: 4, core: 2. Of those that a mesh axis runs over, the one named last changes fastest.
Arguments:
- source: float32 [32, 32, 512], P('gx', 'gy', 'gz'), may hold values from -4.9 to 5.1
- conductivity: float32 [32, 32, 512], P('gx', 'gy', 'gz'), may hold values from 1 to 10
- block_owner: int32 [2, 4, 4], replicated, may hold values from 0 to 15, as said below
Outputs:
- solution: float32 [32, 32, 512], P('gx', 'gy', 'gz')
- residual: float32 [32, 32, 512], P('gx', 'gy', 'gz')
The draws below stay inside these ranges and needn't reach their ends.
Inputs may be any that keep to these rules, and one draw needn't show every extreme that they name: `block_owner`: every aggregate 0 to 15 holds at least one block.
All inputs are finite; a program needn't handle non-finite values.
Results may differ from the reference program's by a relative error of at most 0.0003.
Values sent between devices are 32-bit elements; how exact they have to be, the bound alone decides.
A program may use at most 64 MiB of HBM per device.

```python
import math
import jax
import jax.numpy as jnp
from jax import lax

CX = 16
CY = 8
CZ = 128
GROUPS = 16
SWEEPS = 2
CYCLES = 2
NX = 32
NY = 32
NZ = 512


def draw_source(key, part):
    values = jnp.clip(jax.random.normal(key, (NX, NY, NZ), jnp.float32), -5.0, 5.0) + 0.1
    return values


def draw_block_owner(key, part):
    blocks_x, blocks_y, blocks_z = (NX // CX, NY // CY, NZ // CZ)
    count_all = blocks_x * blocks_y * blocks_z
    seeds = jax.random.permutation(key, count_all)[:GROUPS].astype(jnp.int32)
    every = jnp.arange(count_all, dtype=jnp.int32)
    seed_x = seeds // (blocks_y * blocks_z)
    seed_y = seeds // blocks_z % blocks_y
    seed_z = seeds % blocks_z
    block_x = every // (blocks_y * blocks_z)
    block_y = every // blocks_z % blocks_y
    block_z = every % blocks_z
    distance = jnp.abs(block_x[:, None] - seed_x[None, :]) + jnp.abs(block_y[:, None] - seed_y[None, :]) + jnp.abs(block_z[:, None] - seed_z[None, :])
    scores = distance * GROUPS + jnp.arange(GROUPS, dtype=jnp.int32)[None, :]
    return jnp.argmin(scores, axis=1).astype(jnp.int32).reshape(blocks_x, blocks_y, blocks_z)


def steps_of(rng, extent, cuts, low, top_value):
    loudness, own = 1.0, jax.random.fold_in(rng, 6)
    for dim, parts in cuts:
        heights = jnp.exp(jax.random.uniform(jax.random.fold_in(own, dim), (parts,), jnp.float32, low / len(cuts), top_value / len(cuts)))
        loudness = loudness * jnp.repeat(heights, extent[dim] // parts).reshape([-1 if axis == dim else 1 for axis in range(len(extent))])
    return loudness


def setup_inputs(seed: int = 0) -> dict:
    keys = jax.random.split(jax.random.key(seed), 4)
    return {
        "source": draw_source(jax.random.fold_in(keys[3], 71), 0),
        "conductivity": jnp.clip(jnp.exp(math.log(10.0) - 2.3025851 * jax.random.uniform(keys[1], (NX, NY, NZ), jnp.float32) ** steps_of(keys[1], (NX, NY, NZ), ((0, 2), (1, 4), (2, 4)), -0.2, 0.2)), 1.0, 10.0),
        "block_owner": draw_block_owner(jax.random.fold_in(keys[3], 71), 0),
    }


def face_terms(padded, multiplier):
    face_x = multiplier * (0.5 * (padded[:-1, 1:-1, 1:-1] + padded[1:, 1:-1, 1:-1]))
    face_y = multiplier * (0.5 * (padded[1:-1, :-1, 1:-1] + padded[1:-1, 1:, 1:-1]))
    face_z = multiplier * (0.5 * (padded[1:-1, 1:-1, :-1] + padded[1:-1, 1:-1, 1:]))
    diagonal = face_x[:-1] + face_x[1:] + face_y[:, :-1] + face_y[:, 1:] + face_z[:, :, :-1] + face_z[:, :, 1:]
    return (face_x, face_y, face_z, diagonal)

def stencil(padded, face_x, face_y, face_z, diagonal):
    center = padded[1:-1, 1:-1, 1:-1]
    beside = face_x[1:] * padded[2:, 1:-1, 1:-1] + face_x[:-1] * padded[:-2, 1:-1, 1:-1]
    beside = beside + face_y[:, 1:] * padded[1:-1, 2:, 1:-1] + face_y[:, :-1] * padded[1:-1, :-2, 1:-1]
    beside = beside + face_z[:, :, 1:] * padded[1:-1, 1:-1, 2:] + face_z[:, :, :-1] * padded[1:-1, 1:-1, :-2]
    return diagonal * center - beside

def coarsen(values):
    extent_x, extent_y, extent_z = values.shape
    return values.reshape(extent_x // 2, 2, extent_y // 2, 2, extent_z // 2, 2).sum(axis=(1, 3, 5))

def refine(values):
    extent_x, extent_y, extent_z = values.shape
    spread = jnp.broadcast_to(values[:, None, :, None, :, None], (extent_x, 2, extent_y, 2, extent_z, 2))
    return spread.reshape(2 * extent_x, 2 * extent_y, 2 * extent_z)

def smooth_sweeps(values, target, coeffs, repeats):
    for sweep_index in range(repeats):
        values = values + 0.8 * (target - stencil(jnp.pad(values, 1), *coeffs)) / coeffs[3]
    return values

def reference(source, conductivity, block_owner):
    highest = lax.Precision.HIGHEST
    middle_k = coarsen(conductivity) * 0.125
    coarse_k = coarsen(middle_k) * 0.125
    finest = face_terms(jnp.pad(conductivity, 1, mode='edge'), 1.0)
    middle = face_terms(jnp.pad(middle_k, 1, mode='edge'), 2.0)
    coarse = face_terms(jnp.pad(coarse_k, 1, mode='edge'), 4.0)
    part_x, part_y, part_z = (CX // 4, CY // 4, CZ // 4)
    blocks_x, blocks_y, blocks_z = (NX // CX, NY // CY, NZ // CZ)
    face_x, face_y, face_z, _ = coarse
    member = (block_owner[..., None] == jnp.arange(GROUPS, dtype=jnp.int32)).astype(jnp.float32)
    plane_x = face_x[::part_x].reshape(blocks_x + 1, blocks_y, part_y, blocks_z, part_z).sum(axis=(2, 4))
    plane_y = face_y[:, ::part_y].reshape(blocks_x, part_x, blocks_y + 1, blocks_z, part_z).sum(axis=(1, 4))
    plane_z = face_z[:, :, ::part_z].reshape(blocks_x, part_x, blocks_y, part_y, blocks_z + 1).sum(axis=(1, 3))
    outward = plane_x[:-1] + plane_x[1:] + plane_y[:, :-1] + plane_y[:, 1:] + plane_z[:, :, :-1] + plane_z[:, :, 1:]
    system = jnp.einsum('abcg,abc,abch->gh', member, outward, member, precision=highest)
    coupled = jnp.einsum('abcg,abc,abch->gh', member[:-1], plane_x[1:-1], member[1:], precision=highest)
    coupled = coupled + jnp.einsum('abcg,abc,abch->gh', member[:, :-1], plane_y[:, 1:-1], member[:, 1:], precision=highest)
    coupled = coupled + jnp.einsum('abcg,abc,abch->gh', member[:, :, :-1], plane_z[:, :, 1:-1], member[:, :, 1:], precision=highest)
    factor = jnp.linalg.cholesky(system - coupled - coupled.T)

    def coarse_solve(target):
        level_two = smooth_sweeps(jnp.zeros_like(target), target, coarse, SWEEPS)
        remain = target - stencil(jnp.pad(level_two, 1), *coarse)
        block_sums = remain.reshape(blocks_x, part_x, blocks_y, part_y, blocks_z, part_z).sum(axis=(1, 3, 5))
        group_rhs = jnp.einsum('abcg,abc->g', member, block_sums, precision=highest)
        coarse_sol = jax.scipy.linalg.cho_solve((factor, True), group_rhs)
        lifted = jnp.einsum('abcg,g->abc', member, coarse_sol, precision=highest)
        level_two = (level_two.reshape(blocks_x, part_x, blocks_y, part_y, blocks_z, part_z) + lifted[:, None, :, None, :, None]).reshape(level_two.shape)
        return smooth_sweeps(level_two, target, coarse, SWEEPS)
    solution = jnp.zeros((NX, NY, NZ), jnp.float32)
    for cycle_index in range(CYCLES):
        solution = smooth_sweeps(solution, source, finest, SWEEPS)
        level_rhs = coarsen(source - stencil(jnp.pad(solution, 1), *finest))
        level_one = smooth_sweeps(jnp.zeros_like(level_rhs), level_rhs, middle, SWEEPS)
        next_rhs = coarsen(level_rhs - stencil(jnp.pad(level_one, 1), *middle))
        level_one = level_one + refine(coarse_solve(next_rhs))
        level_one = smooth_sweeps(level_one, level_rhs, middle, SWEEPS)
        solution = solution + refine(level_one)
        solution = smooth_sweeps(solution, source, finest, SWEEPS)
    residual = source - stencil(jnp.pad(solution, 1), *finest)
    return (solution, residual)
```

```python
import functools

import jax
import jax.numpy as jnp
from jax import lax
from jax.experimental import pallas as pl
from jax.experimental.pallas import tpu as pltpu
from jax.sharding import PartitionSpec as P

GROUPS = 16
SWEEPS = 2
CYCLES = 2
F32 = jnp.float32
MESH = pl.DeviceIdType.MESH
HIGHEST = lax.Precision.HIGHEST
AXES = ("gx", "gy", "gz")


def iota(shape, dim):
    return lax.broadcasted_iota(jnp.int32, shape, dim)


def own_faces(u):
    nx = u.shape[0]
    lane, plane = iota(u.shape, 2), iota(u.shape, 0)
    z_low = jnp.sum(jnp.where(lane == plane, u[:, :, 0:1], 0.0), axis=0)
    z_high = jnp.sum(jnp.where(lane == plane, u[:, :, 127:128], 0.0), axis=0)
    y_low = [u[x, 0:1, :] for x in range(nx)]
    y_high = [u[x, 7:8, :] for x in range(nx)]
    return [u[0], u[nx - 1], y_low, y_high, z_low, z_high]


def spread_y(rows):
    return jnp.stack([jnp.broadcast_to(row, (8, 128)) for row in rows])


def spread_z(packed, nx):
    return jnp.stack([jnp.broadcast_to(packed[:, x : x + 1], (8, 128)) for x in range(nx)])


def rolled(u, w):
    s, l = iota(u.shape, 1), iota(u.shape, 2)
    gap = jnp.zeros((1, 8, 128), F32)
    return [
        jnp.concatenate([gap, u[:-1]], axis=0),
        jnp.concatenate([u[1:], gap], axis=0),
        jnp.where(s < w, 0.0, pltpu.roll(u, w, 1)),
        jnp.where(s >= 8 - w, 0.0, pltpu.roll(u, 8 - w, 1)),
        jnp.where(l < w, 0.0, pltpu.roll(u, w, 2)),
        jnp.where(l >= 128 - w, 0.0, pltpu.roll(u, 128 - w, 2)),
    ]


def pair_sum(v, w):
    s, l = iota(v.shape, 1), iota(v.shape, 2)
    v = v + jnp.where(s % (2 * w) < w, pltpu.roll(v, 8 - w, 1), pltpu.roll(v, w, 1))
    return v + jnp.where(l % (2 * w) < w, pltpu.roll(v, 128 - w, 2), pltpu.roll(v, w, 2))


def restrict(v, w):
    v = jnp.stack([v[2 * i] + v[2 * i + 1] for i in range(v.shape[0] // 2)])
    return pair_sum(v, w)


def prolong(v):
    return jnp.stack([v[i // 2] for i in range(2 * v.shape[0])])


def coarse_shifts(v, sx, sy, edge):
    s, l = iota(v.shape, 1), iota(v.shape, 2)
    lz = v.shape[2]
    own = v if edge else jnp.zeros_like(v)
    n = sx * sy

    def across_x(r, down):
        if sx == 1:
            return own
        if down:
            return jnp.concatenate([own[:sy], r[: n - sy]], axis=0)
        return jnp.concatenate([r[sy:], own[n - sy :]], axis=0)

    def across_y(r, down):
        parts = []
        for i in range(sx):
            a, b = i * sy, (i + 1) * sy
            inner = [r[a : b - 1]] if down else [r[a + 1 : b]]
            inner = inner if sy > 1 else []
            parts += ([own[a : a + 1]] + inner) if down else (inner + [own[b - 1 : b]])
        return jnp.concatenate(parts, axis=0)

    up2, down2 = pltpu.roll(v, 2, 1), pltpu.roll(v, 6, 1)
    up1, down1 = pltpu.roll(v, 1, 1), pltpu.roll(v, 7, 1)
    return [
        jnp.where(s < 2, across_x(up2, True), up2),
        jnp.where(s >= 6, across_x(down2, False), down2),
        jnp.where(s % 2 == 0, across_y(down1, True), up1),
        jnp.where(s % 2 == 1, across_y(up1, False), down1),
        jnp.where(l == 0, own, pltpu.roll(v, 1, 2)),
        jnp.where(l == lz - 1, own, pltpu.roll(v, lz - 1, 2)),
    ]


def kernel(sizes, source_ref, k_ref, owner_ref, sol_ref, res_ref,
           sbuf, rbuf, gsend, gbuf, c0, c1, c2, member_ref, wide_ref,
           ssem, rsem, gssem, grsem):
    sx, sy, sz = sizes
    count, n_xy, lz = sx * sy * sz, sx * sy, 32 * sz
    me = [lax.axis_index(a) for a in AXES]
    my_xy = me[0] * sy + me[1]
    linear = my_xy * sz + me[2]
    edge = [me[0] == 0, me[0] == sx - 1, me[1] == 0, me[1] == sy - 1, me[2] == 0, me[2] == sz - 1]

    rbuf[...] = jnp.zeros_like(rbuf)

    def coords(d):
        t = lax.rem(linear + d, count)
        return (t // (sy * sz), (t // sz) % sy, t % sz)

    barrier = pltpu.get_barrier_semaphore()

    @pl.loop(1, count)
    def _(d):
        pl.semaphore_signal(barrier, inc=1, device_id=coords(d), device_id_type=MESH)

    pl.semaphore_wait(barrier, count - 1)

    def copy_of(slot, d, nx):
        axis, step = d // 2, 1 if d % 2 else -1
        there = [me[a] + step if a == axis else me[a] for a in range(3)]
        rows = nx if axis == 1 else 8
        return pltpu.make_async_remote_copy(
            src_ref=sbuf.at[slot, d, pl.ds(0, rows)],
            dst_ref=rbuf.at[slot, d ^ 1, pl.ds(0, rows)],
            send_sem=ssem.at[slot, d],
            recv_sem=rsem.at[slot, d ^ 1],
            device_id=tuple(there),
            device_id_type=MESH,
        )

    def send(slot, faces, nx):
        for d in (4, 5, 2, 3, 0, 1):
            if d in (2, 3):
                for x in range(nx):
                    sbuf[slot, d, x : x + 1, :] = faces[d][x]
            else:
                sbuf[slot, d, 0:8, :] = faces[d]

            @pl.when(jnp.logical_not(edge[d]))
            def _():
                copy_of(slot, d, nx).start()

    def receive(slot, nx):
        for d in range(6):
            @pl.when(jnp.logical_not(edge[d]))
            def _():
                copy = copy_of(slot, d, nx)
                copy.wait_send()
                rows = nx if d // 2 == 1 else 8
                pltpu.make_async_copy(
                    rbuf.at[slot, d, pl.ds(0, rows)], rbuf.at[slot, d, pl.ds(0, rows)],
                    rsem.at[slot, d],
                ).wait()

    def got(slot, nx):
        return [
            [rbuf[slot, d, x : x + 1, :] for x in range(nx)] if d in (2, 3)
            else rbuf[slot, d, 0:8, :]
            for d in range(6)
        ]

    lane_base = (me[2] % 4) * 32

    def gather_copy(use, d):
        return pltpu.make_async_remote_copy(
            src_ref=gsend.at[use],
            dst_ref=gbuf.at[use, linear],
            send_sem=gssem.at[use],
            recv_sem=grsem.at[use],
            device_id=coords(d),
            device_id_type=MESH,
        )

    def gather_start(use, v):
        s = iota((8, 128), 0)
        straight = (s % 2) == (s // 4)
        packed = jnp.zeros((8, 128), F32)
        for x in range(4):
            both = jnp.where(straight, v[x], pltpu.roll(v[x], 4, 0))
            packed = jnp.where(s // 2 == x, both, packed)
        pick = (iota((128, 128), 0) == 4 * (iota((128, 128), 1) - lane_base)).astype(F32)
        packed = jnp.dot(packed, pick, precision=HIGHEST, preferred_element_type=F32)
        gsend[use] = packed
        gbuf[use, linear] = packed

        @pl.loop(1, count)
        def _(d):
            gather_copy(use, d).start()

    def gather_wait(use):
        whole = gbuf.at[use, pl.ds(0, count - 1)]
        pltpu.make_async_copy(whole, whole, gssem.at[use]).wait()
        pltpu.make_async_copy(whole, whole, grsem.at[use]).wait()
        rows = []
        for i in range(n_xy):
            parts = []
            for first in range(0, sz, 4):
                part = gbuf[use, i * sz + first]
                for j in range(first + 1, min(first + 4, sz)):
                    part = part + gbuf[use, i * sz + j]
                parts.append(part)
            rows.append(parts[0] if len(parts) == 1 else jnp.concatenate(parts, axis=1))
        return jnp.stack(rows)

    def set_up(c_ref, k, faces, halo, w):
        nx = k.shape[0]
        beside = rolled(k, w)
        shape = k.shape
        p, s, l = iota(shape, 0), iota(shape, 1), iota(shape, 2)
        masks = [p < 1, p >= nx - 1, s < w, s >= 8 - w, l < w, l >= 128 - w]
        total = jnp.zeros(shape, F32)
        for d in range(6):
            if d in (2, 3):
                far = spread_y([jnp.where(edge[d], a, b) for a, b in zip(faces[d], halo[d])])
            else:
                far = jnp.where(edge[d], faces[d], halo[d])
                far = spread_z(far, nx) if d >= 4 else jnp.broadcast_to(far[None], shape)
            c = float(w) * (0.5 * (k + jnp.where(masks[d], far, beside[d])))
            c_ref[d] = c
            total = total + c
        c_ref[6] = total
        c_ref[7] = 0.8 / total

    k0 = k_ref[...]
    k0_faces = own_faces(k0)
    send(0, k0_faces, 16)
    k1 = restrict(k0, 1) * 0.125
    k1_faces = own_faces(k1)
    send(1, k1_faces, 8)
    k2 = restrict(k1, 2) * 0.125
    gather_start(0, k2)

    receive(0, 16)
    set_up(c0, k0, k0_faces, got(0, 16), 1)
    receive(1, 8)
    set_up(c1, k1, k1_faces, got(1, 8), 2)

    phase = [0]

    def residual(c_ref, u, b, w, beside_wait=None):
        nx = u.shape[0]
        slot = 2 + phase[0] % 2
        phase[0] += 1
        send(slot, own_faces(u), nx)
        inner = rolled(u, w)
        r = b - c_ref[6] * u
        for d in range(6):
            r = r + c_ref[d] * inner[d]
        if beside_wait is not None:
            beside_wait()
        receive(slot, nx)
        halo = got(slot, nx)
        s, l = iota(u.shape, 1), iota(u.shape, 2)
        r = r + jnp.where(s < w, c_ref[2] * spread_y(halo[2]), 0.0)
        r = r + jnp.where(s >= 8 - w, c_ref[3] * spread_y(halo[3]), 0.0)
        r = r + jnp.where(l < w, c_ref[4] * spread_z(halo[4], nx), 0.0)
        r = r + jnp.where(l >= 128 - w, c_ref[5] * spread_z(halo[5], nx), 0.0)
        low = r[0] + c_ref[0, 0] * halo[0]
        high = r[nx - 1] + c_ref[1, nx - 1] * halo[1]
        return jnp.concatenate([low[None], r[1:-1], high[None]], axis=0)

    def sweep(c_ref, u, b, w):
        return u + c_ref[7] * residual(c_ref, u, b, w)

    def coarse_residual(v, b):
        beside = coarse_shifts(v, sx, sy, False)
        r = b - c2[6] * v
        for d in range(6):
            r = r + c2[d] * beside[d]
        return r

    def coarse_sweep(v, b):
        return v + c2[7] * coarse_residual(v, b)

    def coarse_set_up():
        k = gather_wait(0)
        beside = coarse_shifts(k, sx, sy, True)
        total = jnp.zeros_like(k)
        faces = []
        for d in range(6):
            c = 4.0 * (0.5 * (k + beside[d]))
            c2[d] = c
            faces.append(c)
            total = total + c
        c2[6] = total
        c2[7] = 0.8 / total
        s, l = iota(k.shape, 1), iota(k.shape, 2)
        outer = [s < 2, s >= 6, s % 2 == 0, s % 2 == 1, l % 32 == 0, l % 32 == 31]
        outward = [
            jnp.sum(jnp.where(m, c, 0.0), axis=1, keepdims=True) for m, c in zip(outer, faces)
        ]
        block = iota((1, lz), 1) // 32

        def owners(i, j, shift):
            row = jnp.full((1, lz), -1, jnp.int32)
            if not (0 <= i < sx and 0 <= j < sy):
                return row
            for z in range(sz):
                if 0 <= z + shift < sz:
                    row = jnp.where(block == z, owner_ref[i, j, z + shift], row)
            return row

        label = iota((GROUPS, lz), 0)
        system = jnp.zeros((GROUPS, GROUPS), F32)
        for i in range(sx):
            for j in range(sy):
                at = i * sy + j
                mine = owners(i, j, 0) == label
                member = jnp.where(mine, 1.0, 0.0)
                member_ref[at] = member
                out = [o[at] for o in outward]
                terms = jnp.where(mine, out[0] + out[1] + out[2] + out[3] + out[4] + out[5], 0.0)
                near = [(i - 1, j, 0), (i + 1, j, 0), (i, j - 1, 0), (i, j + 1, 0),
                        (i, j, -1), (i, j, 1)]
                for d in range(6):
                    terms = terms - jnp.where(owners(*near[d]) == label, out[d], 0.0)
                system = system + lax.dot_general(
                    member, terms, (((1,), (1,)), ((), ())), precision=HIGHEST,
                    preferred_element_type=F32)
        rows, columns = iota((GROUPS, GROUPS), 0), iota((GROUPS, GROUPS), 1)

        def eliminate(step, a):
            at_row, at_column = rows == step, columns == step
            row = jnp.sum(jnp.where(at_row, a, 0.0), axis=0, keepdims=True)
            column = jnp.sum(jnp.where(at_column, a, 0.0), axis=1, keepdims=True)
            pivot = jnp.sum(jnp.where(at_column, row, 0.0), axis=1, keepdims=True)
            over = 1.0 / pivot[0:1]
            swept = a - column * (row * over)
            swept = jnp.where(at_row, row * over, swept)
            swept = jnp.where(at_column, column * over, swept)
            return jnp.where(at_row & at_column, -over, swept)

        return -lax.fori_loop(0, GROUPS, eliminate, system)

    diagonal = iota((GROUPS, GROUPS), 0) == iota((GROUPS, GROUPS), 1)

    def coarse_solve(b, inverse):
        v = c2[7] * b
        for _ in range(SWEEPS - 1):
            v = coarse_sweep(v, b)
        sums = jnp.sum(coarse_residual(v, b), axis=1, keepdims=True)
        grouped = jnp.zeros((GROUPS, lz), F32)
        for i in range(n_xy):
            grouped = grouped + member_ref[i] * sums[i]
        rc = jnp.sum(grouped, axis=1, keepdims=True)
        xc = jnp.sum(inverse * rc, axis=0, keepdims=True)
        xc = jnp.sum(jnp.where(diagonal, xc, 0.0), axis=1, keepdims=True)
        lifted = jnp.stack([
            jnp.sum(member_ref[i] * xc, axis=0, keepdims=True) for i in range(n_xy)
        ])
        v = v + lifted
        for _ in range(SWEEPS):
            v = coarse_sweep(v, b)
        for first in range(lz // 128):
            wide_ref[:, first] = v[:, :, first * 128 : first * 128 + 128]
        mine = wide_ref[my_xy, me[2] // 4]
        put = (iota((128, 128), 0) == lane_base + iota((128, 128), 1) // 4).astype(F32)
        mine = jnp.dot(mine, put, precision=HIGHEST, preferred_element_type=F32)
        low = iota((8, 128), 0) < 4
        return jnp.stack([
            jnp.where(low, mine[2 * x : 2 * x + 1], mine[2 * x + 1 : 2 * x + 2])
            for x in range(4)
        ])

    source = source_ref[...]
    inverse = None
    u = None
    for cycle in range(CYCLES):
        if cycle == 0:
            u = c0[7] * source
        else:
            u = sweep(c0, u, source, 1)
        for _ in range(SWEEPS - 1):
            u = sweep(c0, u, source, 1)
        b1 = restrict(residual(c0, u, source, 1), 1)
        u1 = c1[7] * b1
        for _ in range(SWEEPS - 1):
            u1 = sweep(c1, u1, b1, 2)
        b2 = restrict(residual(c1, u1, b1, 2), 2)
        gather_start(1 + cycle, b2)
        if cycle == 0:
            inverse = coarse_set_up()
        u1 = u1 + prolong(coarse_solve(gather_wait(1 + cycle), inverse))
        for _ in range(SWEEPS):
            u1 = sweep(c1, u1, b1, 2)
        u = u + prolong(u1)
        for _ in range(SWEEPS):
            u = sweep(c0, u, source, 1)
    sol_ref[...] = u
    res_ref[...] = residual(c0, u, source, 1)


def solution(mesh):
    sizes = tuple(mesh.shape[a] for a in AXES)
    sx, sy, sz = sizes
    count, n_xy, lz = sx * sy * sz, sx * sy, 32 * sz

    def on_device(source, conductivity, block_owner):
        vmem = pl.BlockSpec(memory_space=pltpu.VMEM)
        return pl.pallas_call(
            functools.partial(kernel, sizes),
            out_shape=[jax.ShapeDtypeStruct(source.shape, F32)] * 2,
            in_specs=[vmem, vmem, pl.BlockSpec(memory_space=pltpu.SMEM)],
            out_specs=[vmem, vmem],
            scratch_shapes=[
                pltpu.VMEM((4, 6, 16, 128), F32),
                pltpu.VMEM((4, 6, 16, 128), F32),
                pltpu.VMEM((3, 8, 128), F32),
                pltpu.VMEM((3, count, 8, 128), F32),
                pltpu.VMEM((8, 16, 8, 128), F32),
                pltpu.VMEM((8, 8, 8, 128), F32),
                pltpu.VMEM((8, n_xy, 8, lz), F32),
                pltpu.VMEM((n_xy, GROUPS, lz), F32),
                pltpu.VMEM((n_xy, lz // 128, 8, 128), F32),
                pltpu.SemaphoreType.DMA((4, 6)),
                pltpu.SemaphoreType.DMA((4, 6)),
                pltpu.SemaphoreType.DMA((3,)),
                pltpu.SemaphoreType.DMA((3,)),
            ],
            compiler_params=pltpu.CompilerParams(
                collective_id=0, has_side_effects=True, vmem_limit_bytes=48 * 1024 * 1024
            ),
        )(source, conductivity, block_owner)

    spec = P(*AXES)
    return jax.shard_map(
        on_device, mesh=mesh, in_specs=(spec, spec, P()), out_specs=(spec, spec), check_vma=False
    )
```

```python
import functools

import jax
import jax.numpy as jnp
from jax import lax
from jax.experimental import pallas as pl
from jax.experimental.pallas import tpu as pltpu
from jax.sharding import PartitionSpec as P

GROUPS = 16
SWEEPS = 2
CYCLES = 2
F32 = jnp.float32
MESH = pl.DeviceIdType.MESH
HIGHEST = lax.Precision.HIGHEST
AXES = ("gx", "gy", "gz")


def iota(shape, dim):
    return lax.broadcasted_iota(jnp.int32, shape, dim)


def own_faces(u):
    nx = u.shape[0]
    lane, plane = iota(u.shape, 2), iota(u.shape, 0)
    z_low = jnp.sum(jnp.where(lane == plane, u[:, :, 0:1], 0.0), axis=0)
    z_high = jnp.sum(jnp.where(lane == plane, u[:, :, 127:128], 0.0), axis=0)
    y_low = [u[x, 0:1, :] for x in range(nx)]
    y_high = [u[x, 7:8, :] for x in range(nx)]
    return [u[0], u[nx - 1], y_low, y_high, z_low, z_high]


def spread_y(rows):
    return jnp.stack([jnp.broadcast_to(row, (8, 128)) for row in rows])


def spread_z(packed, nx):
    return jnp.stack([jnp.broadcast_to(packed[:, x : x + 1], (8, 128)) for x in range(nx)])


def rolled(u, w):
    s, l = iota(u.shape, 1), iota(u.shape, 2)
    gap = jnp.zeros((1, 8, 128), F32)
    return [
        jnp.concatenate([gap, u[:-1]], axis=0),
        jnp.concatenate([u[1:], gap], axis=0),
        jnp.where(s < w, 0.0, pltpu.roll(u, w, 1)),
        jnp.where(s >= 8 - w, 0.0, pltpu.roll(u, 8 - w, 1)),
        jnp.where(l < w, 0.0, pltpu.roll(u, w, 2)),
        jnp.where(l >= 128 - w, 0.0, pltpu.roll(u, 128 - w, 2)),
    ]


def pair_sum(v, w):
    s, l = iota(v.shape, 1), iota(v.shape, 2)
    v = v + jnp.where(s % (2 * w) < w, pltpu.roll(v, 8 - w, 1), pltpu.roll(v, w, 1))
    return v + jnp.where(l % (2 * w) < w, pltpu.roll(v, 128 - w, 2), pltpu.roll(v, w, 2))


def restrict(v, w):
    v = jnp.stack([v[2 * i] + v[2 * i + 1] for i in range(v.shape[0] // 2)])
    return pair_sum(v, w)


def prolong(v):
    return jnp.stack([v[i // 2] for i in range(2 * v.shape[0])])


def coarse_shifts(v, sx, sy, edge):
    s, l = iota(v.shape, 1), iota(v.shape, 2)
    lz = v.shape[2]
    own = v if edge else jnp.zeros_like(v)
    n = sx * sy

    def across_x(r, down):
        if sx == 1:
            return own
        if down:
            return jnp.concatenate([own[:sy], r[: n - sy]], axis=0)
        return jnp.concatenate([r[sy:], own[n - sy :]], axis=0)

    def across_y(r, down):
        parts = []
        for i in range(sx):
            a, b = i * sy, (i + 1) * sy
            inner = [r[a : b - 1]] if down else [r[a + 1 : b]]
            inner = inner if sy > 1 else []
            parts += ([own[a : a + 1]] + inner) if down else (inner + [own[b - 1 : b]])
        return jnp.concatenate(parts, axis=0)

    up2, down2 = pltpu.roll(v, 2, 1), pltpu.roll(v, 6, 1)
    up1, down1 = pltpu.roll(v, 1, 1), pltpu.roll(v, 7, 1)
    return [
        jnp.where(s < 2, across_x(up2, True), up2),
        jnp.where(s >= 6, across_x(down2, False), down2),
        jnp.where(s % 2 == 0, across_y(down1, True), up1),
        jnp.where(s % 2 == 1, across_y(up1, False), down1),
        jnp.where(l == 0, own, pltpu.roll(v, 1, 2)),
        jnp.where(l == lz - 1, own, pltpu.roll(v, lz - 1, 2)),
    ]


def kernel(sizes, source_ref, k_ref, owner_ref, sol_ref, res_ref,
           sbuf, rbuf, zbuf, gbuf, c0, c1, c2, member_ref, wide_ref, matrix_ref,
           ssem, rsem, zssem, zrsem, gssem, grsem):
    sx, sy, sz = sizes
    n_xy, lz = sx * sy, 32 * sz
    me = [lax.axis_index(a) for a in AXES]
    my_xy = me[0] * sy + me[1]
    edge = [me[0] == 0, me[0] == sx - 1, me[1] == 0, me[1] == sy - 1, me[2] == 0, me[2] == sz - 1]

    rbuf[...] = jnp.zeros_like(rbuf)

    def line_peer(d):
        t = me[2] + d
        return (me[0], me[1], jnp.where(t >= sz, t - sz, t))

    def plane_peer(d):
        t = my_xy + d
        t = jnp.where(t >= n_xy, t - n_xy, t)
        return (t // sy, t % sy, me[2])

    def over_plane(body):
        if n_xy <= 8:
            for d in range(1, n_xy):
                body(d)
        else:
            pl.loop(1, n_xy)(body)

    barrier = pltpu.get_barrier_semaphore()

    def greet(there):
        pl.semaphore_signal(barrier, inc=1, device_id=there, device_id_type=MESH)

    for d in range(1, sz):
        greet(line_peer(d))
    over_plane(lambda d: greet(plane_peer(d)))
    pl.semaphore_wait(barrier, sz - 1 + n_xy - 1)

    def copy_of(slot, d, nx):
        axis, step = d // 2, 1 if d % 2 else -1
        there = [me[a] + step if a == axis else me[a] for a in range(3)]
        rows = nx if axis == 1 else 8
        return pltpu.make_async_remote_copy(
            src_ref=sbuf.at[slot, d, pl.ds(0, rows)],
            dst_ref=rbuf.at[slot, d ^ 1, pl.ds(0, rows)],
            send_sem=ssem.at[slot, d],
            recv_sem=rsem.at[slot, d ^ 1],
            device_id=tuple(there),
            device_id_type=MESH,
        )

    def send(slot, faces, nx):
        for d in (4, 5, 2, 3, 0, 1):
            if d in (2, 3):
                for x in range(nx):
                    sbuf[slot, d, x : x + 1, :] = faces[d][x]
            else:
                sbuf[slot, d, 0:8, :] = faces[d]

        for d in (4, 5, 2, 3, 0, 1):
            @pl.when(jnp.logical_not(edge[d]))
            def _():
                copy_of(slot, d, nx).start()

    def receive(slot, nx):
        for d in range(6):
            @pl.when(jnp.logical_not(edge[d]))
            def _():
                copy = copy_of(slot, d, nx)
                copy.wait_send()
                rows = nx if d // 2 == 1 else 8
                pltpu.make_async_copy(
                    rbuf.at[slot, d, pl.ds(0, rows)], rbuf.at[slot, d, pl.ds(0, rows)],
                    rsem.at[slot, d],
                ).wait()

    def got(slot, nx):
        return [
            [rbuf[slot, d, x : x + 1, :] for x in range(nx)] if d in (2, 3)
            else rbuf[slot, d, 0:8, :]
            for d in range(6)
        ]

    lane_base = (me[2] % 4) * 32

    def line_copy(use, d):
        return pltpu.make_async_remote_copy(
            src_ref=zbuf.at[use, me[2]],
            dst_ref=zbuf.at[use, me[2]],
            send_sem=zssem.at[use],
            recv_sem=zrsem.at[use],
            device_id=line_peer(d),
            device_id_type=MESH,
        )

    def plane_copy(use, d):
        return pltpu.make_async_remote_copy(
            src_ref=gbuf.at[use, my_xy],
            dst_ref=gbuf.at[use, my_xy],
            send_sem=gssem.at[use],
            recv_sem=grsem.at[use],
            device_id=plane_peer(d),
            device_id_type=MESH,
        )

    def await_all(ref, send_sem, recv_sem):
        pltpu.make_async_copy(ref, ref, send_sem).wait()
        pltpu.make_async_copy(ref, ref, recv_sem).wait()

    def gather_start(use, v):
        s = iota((8, 128), 0)
        straight = (s % 2) == (s // 4)
        packed = jnp.zeros((8, 128), F32)
        for x in range(4):
            both = jnp.where(straight, v[x], pltpu.roll(v[x], 4, 0))
            packed = jnp.where(s // 2 == x, both, packed)
        pick = (iota((128, 128), 0) == 4 * (iota((128, 128), 1) - lane_base)).astype(F32)
        packed = jnp.dot(packed, pick, precision=HIGHEST, preferred_element_type=F32)
        zbuf[use, me[2]] = packed
        for d in range(1, sz):
            line_copy(use, d).start()

    def gather_next(use):
        await_all(zbuf.at[use, pl.ds(0, sz - 1)], zssem.at[use], zrsem.at[use])
        for group in range(lz // 128):
            part = zbuf[use, 4 * group]
            for j in range(4 * group + 1, 4 * group + 4):
                part = part + zbuf[use, j]
            gbuf[use, my_xy, group] = part
        over_plane(lambda d: plane_copy(use, d).start())

    def gather_wait(use):
        await_all(gbuf.at[use, pl.ds(0, n_xy - 1)], gssem.at[use], grsem.at[use])
        rows = []
        for i in range(n_xy):
            parts = [gbuf[use, i, group] for group in range(lz // 128)]
            rows.append(parts[0] if len(parts) == 1 else jnp.concatenate(parts, axis=1))
        return jnp.stack(rows)

    def set_up(c_ref, k, faces, halo, w):
        nx = k.shape[0]
        beside = rolled(k, w)
        shape = k.shape
        p, s, l = iota(shape, 0), iota(shape, 1), iota(shape, 2)
        masks = [p < 1, p >= nx - 1, s < w, s >= 8 - w, l < w, l >= 128 - w]
        total = jnp.zeros(shape, F32)
        for d in range(6):
            if d in (2, 3):
                far = spread_y([jnp.where(edge[d], a, b) for a, b in zip(faces[d], halo[d])])
            else:
                far = jnp.where(edge[d], faces[d], halo[d])
                far = spread_z(far, nx) if d >= 4 else jnp.broadcast_to(far[None], shape)
            c = float(w) * (0.5 * (k + jnp.where(masks[d], far, beside[d])))
            c_ref[d] = c
            total = total + c
        c_ref[6] = total
        c_ref[7] = 0.8 / total

    k0 = k_ref[...]
    k0_faces = own_faces(k0)
    send(0, k0_faces, 16)
    k1 = restrict(k0, 1) * 0.125
    k1_faces = own_faces(k1)
    send(1, k1_faces, 8)
    k2 = restrict(k1, 2) * 0.125
    gather_start(0, k2)

    receive(0, 16)
    set_up(c0, k0, k0_faces, got(0, 16), 1)
    receive(1, 8)
    gather_next(0)
    set_up(c1, k1, k1_faces, got(1, 8), 2)

    phase = [0]

    def residual(c_ref, u, b, w, beside_wait=None):
        nx = u.shape[0]
        slot = 2 + phase[0] % 2
        phase[0] += 1
        send(slot, own_faces(u), nx)
        inner = rolled(u, w)
        r = b - c_ref[6] * u
        for d in range(6):
            r = r + c_ref[d] * inner[d]
        if beside_wait is not None:
            beside_wait()
        receive(slot, nx)
        halo = got(slot, nx)
        s, l = iota(u.shape, 1), iota(u.shape, 2)
        r = r + jnp.where(s < w, c_ref[2] * spread_y(halo[2]), 0.0)
        r = r + jnp.where(s >= 8 - w, c_ref[3] * spread_y(halo[3]), 0.0)
        r = r + jnp.where(l < w, c_ref[4] * spread_z(halo[4], nx), 0.0)
        r = r + jnp.where(l >= 128 - w, c_ref[5] * spread_z(halo[5], nx), 0.0)
        low = r[0] + c_ref[0, 0] * halo[0]
        high = r[nx - 1] + c_ref[1, nx - 1] * halo[1]
        return jnp.concatenate([low[None], r[1:-1], high[None]], axis=0)

    def sweep(c_ref, u, b, w, beside_wait=None):
        return u + c_ref[7] * residual(c_ref, u, b, w, beside_wait)

    def coarse_residual(v, b):
        beside = coarse_shifts(v, sx, sy, False)
        r = b - c2[6] * v
        for d in range(6):
            r = r + c2[d] * beside[d]
        return r

    def coarse_sweep(v, b):
        return v + c2[7] * coarse_residual(v, b)

    def coarse_set_up():
        k = gather_wait(0)
        beside = coarse_shifts(k, sx, sy, True)
        total = jnp.zeros_like(k)
        faces = []
        for d in range(6):
            c = 4.0 * (0.5 * (k + beside[d]))
            c2[d] = c
            faces.append(c)
            total = total + c
        c2[6] = total
        c2[7] = 0.8 / total
        s, l = iota(k.shape, 1), iota(k.shape, 2)
        outer = [s < 2, s >= 6, s % 2 == 0, s % 2 == 1, l % 32 == 0, l % 32 == 31]
        outward = [
            jnp.sum(jnp.where(m, c, 0.0), axis=1, keepdims=True) for m, c in zip(outer, faces)
        ]
        block = iota((1, lz), 1) // 32

        def owners(i, j, shift):
            row = jnp.full((1, lz), -1, jnp.int32)
            if not (0 <= i < sx and 0 <= j < sy):
                return row
            for z in range(sz):
                if 0 <= z + shift < sz:
                    row = jnp.where(block == z, owner_ref[i, j, z + shift], row)
            return row

        label = iota((GROUPS, lz), 0)
        system = jnp.zeros((GROUPS, GROUPS), F32)
        for i in range(sx):
            for j in range(sy):
                at = i * sy + j
                mine = owners(i, j, 0) == label
                member = jnp.where(mine, 1.0, 0.0)
                member_ref[at] = member
                out = [o[at] for o in outward]
                terms = jnp.where(mine, out[0] + out[1] + out[2] + out[3] + out[4] + out[5], 0.0)
                near = [(i - 1, j, 0), (i + 1, j, 0), (i, j - 1, 0), (i, j + 1, 0),
                        (i, j, -1), (i, j, 1)]
                for d in range(6):
                    terms = terms - jnp.where(owners(*near[d]) == label, out[d], 0.0)
                system = system + lax.dot_general(
                    member, terms, (((1,), (1,)), ((), ())), precision=HIGHEST,
                    preferred_element_type=F32)
        matrix_ref[...] = system

    def eliminate(first, last):
        rows, columns = iota((GROUPS, GROUPS), 0), iota((GROUPS, GROUPS), 1)
        a = matrix_ref[...]
        for step in range(first, last):
            at_row, at_column = rows == step, columns == step
            over = 1.0 / jnp.broadcast_to(a[step : step + 1, step : step + 1], (1, GROUPS))
            row = a[step : step + 1, :] * over
            column = jnp.broadcast_to(a[:, step : step + 1], (GROUPS, GROUPS))
            swept = jnp.where(at_column, column * over, a - column * row)
            a = jnp.where(at_row, jnp.where(at_column, -over, row), swept)
        matrix_ref[...] = a

    diagonal = iota((GROUPS, GROUPS), 0) == iota((GROUPS, GROUPS), 1)

    def coarse_solve(b, inverse):
        v = c2[7] * b
        for _ in range(SWEEPS - 1):
            v = coarse_sweep(v, b)
        sums = jnp.sum(coarse_residual(v, b), axis=1, keepdims=True)
        grouped = jnp.zeros((GROUPS, lz), F32)
        for i in range(n_xy):
            grouped = grouped + member_ref[i] * sums[i]
        rc = jnp.sum(grouped, axis=1, keepdims=True)
        xc = jnp.sum(inverse * rc, axis=0, keepdims=True)
        xc = jnp.sum(jnp.where(diagonal, xc, 0.0), axis=1, keepdims=True)
        lifted = jnp.stack([
            jnp.sum(member_ref[i] * xc, axis=0, keepdims=True) for i in range(n_xy)
        ])
        v = v + lifted
        for _ in range(SWEEPS):
            v = coarse_sweep(v, b)
        for first in range(lz // 128):
            wide_ref[:, first] = v[:, :, first * 128 : first * 128 + 128]
        mine = wide_ref[my_xy, me[2] // 4]
        put = (iota((128, 128), 0) == lane_base + iota((128, 128), 1) // 4).astype(F32)
        mine = jnp.dot(mine, put, precision=HIGHEST, preferred_element_type=F32)
        low = iota((8, 128), 0) < 4
        return jnp.stack([
            jnp.where(low, mine[2 * x : 2 * x + 1], mine[2 * x + 1 : 2 * x + 2])
            for x in range(4)
        ])

    def part(first, last):
        return lambda: eliminate(first, last)

    source = source_ref[...]
    u = None
    for cycle in range(CYCLES):
        first = cycle == 0
        u = c0[7] * source if first else sweep(c0, u, source, 1)
        u = sweep(c0, u, source, 1, coarse_set_up if first else None)
        b1 = restrict(residual(c0, u, source, 1, part(0, 4) if first else None), 1)
        u1 = c1[7] * b1
        u1 = sweep(c1, u1, b1, 2, part(4, 8) if first else None)
        b2 = restrict(residual(c1, u1, b1, 2, part(8, 12) if first else None), 2)
        gather_start(1 + cycle, b2)
        if first:
            eliminate(12, 14)
        gather_next(1 + cycle)
        if first:
            eliminate(14, 16)
        u1 = u1 + prolong(coarse_solve(gather_wait(1 + cycle), -matrix_ref[...]))
        for _ in range(SWEEPS):
            u1 = sweep(c1, u1, b1, 2)
        u = u + prolong(u1)
        for _ in range(SWEEPS):
            u = sweep(c0, u, source, 1)
    sol_ref[...] = u
    res_ref[...] = residual(c0, u, source, 1)


def solution(mesh):
    sizes = tuple(mesh.shape[a] for a in AXES)
    sx, sy, sz = sizes
    n_xy, lz = sx * sy, 32 * sz

    def on_device(source, conductivity, block_owner):
        vmem = pl.BlockSpec(memory_space=pltpu.VMEM)
        return pl.pallas_call(
            functools.partial(kernel, sizes),
            out_shape=[jax.ShapeDtypeStruct(source.shape, F32)] * 2,
            in_specs=[vmem, vmem, pl.BlockSpec(memory_space=pltpu.SMEM)],
            out_specs=[vmem, vmem],
            scratch_shapes=[
                pltpu.VMEM((4, 6, 16, 128), F32),
                pltpu.VMEM((4, 6, 16, 128), F32),
                pltpu.VMEM((3, sz, 8, 128), F32),
                pltpu.VMEM((3, n_xy, lz // 128, 8, 128), F32),
                pltpu.VMEM((8, 16, 8, 128), F32),
                pltpu.VMEM((8, 8, 8, 128), F32),
                pltpu.VMEM((8, n_xy, 8, lz), F32),
                pltpu.VMEM((n_xy, GROUPS, lz), F32),
                pltpu.VMEM((n_xy, lz // 128, 8, 128), F32),
                pltpu.VMEM((GROUPS, GROUPS), F32),
                pltpu.SemaphoreType.DMA((4, 6)),
                pltpu.SemaphoreType.DMA((4, 6)),
                pltpu.SemaphoreType.DMA((3,)),
                pltpu.SemaphoreType.DMA((3,)),
                pltpu.SemaphoreType.DMA((3,)),
                pltpu.SemaphoreType.DMA((3,)),
            ],
            compiler_params=pltpu.CompilerParams(
                collective_id=0, has_side_effects=True, vmem_limit_bytes=48 * 1024 * 1024
            ),
        )(source, conductivity, block_owner)

    spec = P(*AXES)
    return jax.shard_map(
        on_device, mesh=mesh, in_specs=(spec, spec, P()), out_specs=(spec, spec), check_vma=False
    )
```

```python
import functools

import jax
import jax.numpy as jnp
from jax import lax
from jax.experimental import pallas as pl
from jax.experimental.pallas import tpu as pltpu
from jax.sharding import PartitionSpec as P

GROUPS = 16
SWEEPS = 2
CYCLES = 2
F32 = jnp.float32
MESH = pl.DeviceIdType.MESH
HIGHEST = lax.Precision.HIGHEST
AXES = ("gx", "gy", "gz")


def iota(shape, dim):
    return lax.broadcasted_iota(jnp.int32, shape, dim)


def own_faces(u):
    nx = u.shape[0]
    lane, plane = iota(u.shape, 2), iota(u.shape, 0)
    z_low = jnp.sum(jnp.where(lane == plane, u[:, :, 0:1], 0.0), axis=0)
    z_high = jnp.sum(jnp.where(lane == plane, u[:, :, 127:128], 0.0), axis=0)
    y_low = [u[x, 0:1, :] for x in range(nx)]
    y_high = [u[x, 7:8, :] for x in range(nx)]
    return [u[0], u[nx - 1], y_low, y_high, z_low, z_high]


def spread_y(rows):
    return jnp.stack([jnp.broadcast_to(row, (8, 128)) for row in rows])


def spread_z(packed, nx):
    return jnp.stack([jnp.broadcast_to(packed[:, x : x + 1], (8, 128)) for x in range(nx)])


def rolled(u, w):
    s, l = iota(u.shape, 1), iota(u.shape, 2)
    gap = jnp.zeros((1, 8, 128), F32)
    return [
        jnp.concatenate([gap, u[:-1]], axis=0),
        jnp.concatenate([u[1:], gap], axis=0),
        jnp.where(s < w, 0.0, pltpu.roll(u, w, 1)),
        jnp.where(s >= 8 - w, 0.0, pltpu.roll(u, 8 - w, 1)),
        jnp.where(l < w, 0.0, pltpu.roll(u, w, 2)),
        jnp.where(l >= 128 - w, 0.0, pltpu.roll(u, 128 - w, 2)),
    ]


def pair_sum(v, w):
    s, l = iota(v.shape, 1), iota(v.shape, 2)
    v = v + jnp.where(s % (2 * w) < w, pltpu.roll(v, 8 - w, 1), pltpu.roll(v, w, 1))
    return v + jnp.where(l % (2 * w) < w, pltpu.roll(v, 128 - w, 2), pltpu.roll(v, w, 2))


def restrict(v, w):
    v = jnp.stack([v[2 * i] + v[2 * i + 1] for i in range(v.shape[0] // 2)])
    return pair_sum(v, w)


def prolong(v):
    return jnp.stack([v[i // 2] for i in range(2 * v.shape[0])])


def coarse_shifts(v, sx, sy, edge):
    s, l = iota(v.shape, 1), iota(v.shape, 2)
    lz = v.shape[2]
    own = v if edge else jnp.zeros_like(v)
    n = sx * sy

    def across_x(r, down):
        if sx == 1:
            return own
        if down:
            return jnp.concatenate([own[:sy], r[: n - sy]], axis=0)
        return jnp.concatenate([r[sy:], own[n - sy :]], axis=0)

    def across_y(r, down):
        parts = []
        for i in range(sx):
            a, b = i * sy, (i + 1) * sy
            inner = [r[a : b - 1]] if down else [r[a + 1 : b]]
            inner = inner if sy > 1 else []
            parts += ([own[a : a + 1]] + inner) if down else (inner + [own[b - 1 : b]])
        return jnp.concatenate(parts, axis=0)

    up2, down2 = pltpu.roll(v, 2, 1), pltpu.roll(v, 6, 1)
    up1, down1 = pltpu.roll(v, 1, 1), pltpu.roll(v, 7, 1)
    return [
        jnp.where(s < 2, across_x(up2, True), up2),
        jnp.where(s >= 6, across_x(down2, False), down2),
        jnp.where(s % 2 == 0, across_y(down1, True), up1),
        jnp.where(s % 2 == 1, across_y(up1, False), down1),
        jnp.where(l == 0, own, pltpu.roll(v, 1, 2)),
        jnp.where(l == lz - 1, own, pltpu.roll(v, lz - 1, 2)),
    ]


def kernel(sizes, source_ref, k_ref, owner_ref, sol_ref, res_ref,
           sbuf, rbuf, gsend, gbuf, c0, c1, c2, member_ref, wide_ref, matrix_ref,
           ssem, rsem, gssem, grsem):
    sx, sy, sz = sizes
    count, n_xy, lz = sx * sy * sz, sx * sy, 32 * sz
    me = [lax.axis_index(a) for a in AXES]
    my_xy = me[0] * sy + me[1]
    linear = my_xy * sz + me[2]
    edge = [me[0] == 0, me[0] == sx - 1, me[1] == 0, me[1] == sy - 1, me[2] == 0, me[2] == sz - 1]

    rbuf[...] = jnp.zeros_like(rbuf)

    def coords(d):
        t = lax.rem(linear + d, count)
        return (t // (sy * sz), (t // sz) % sy, t % sz)

    barrier = pltpu.get_barrier_semaphore()

    @pl.loop(1, count)
    def _(d):
        pl.semaphore_signal(barrier, inc=1, device_id=coords(d), device_id_type=MESH)

    pl.semaphore_wait(barrier, count - 1)

    def copy_of(slot, d, nx):
        axis, step = d // 2, 1 if d % 2 else -1
        there = [me[a] + step if a == axis else me[a] for a in range(3)]
        rows = nx if axis == 1 else 8
        return pltpu.make_async_remote_copy(
            src_ref=sbuf.at[slot, d, pl.ds(0, rows)],
            dst_ref=rbuf.at[slot, d ^ 1, pl.ds(0, rows)],
            send_sem=ssem.at[slot, d],
            recv_sem=rsem.at[slot, d ^ 1],
            device_id=tuple(there),
            device_id_type=MESH,
        )

    def send(slot, faces, nx):
        for d in (4, 5, 2, 3, 0, 1):
            if d in (2, 3):
                for x in range(nx):
                    sbuf[slot, d, x : x + 1, :] = faces[d][x]
            else:
                sbuf[slot, d, 0:8, :] = faces[d]

            @pl.when(jnp.logical_not(edge[d]))
            def _():
                copy_of(slot, d, nx).start()

    def receive(slot, nx):
        for d in range(6):
            @pl.when(jnp.logical_not(edge[d]))
            def _():
                copy = copy_of(slot, d, nx)
                copy.wait_send()
                rows = nx if d // 2 == 1 else 8
                pltpu.make_async_copy(
                    rbuf.at[slot, d, pl.ds(0, rows)], rbuf.at[slot, d, pl.ds(0, rows)],
                    rsem.at[slot, d],
                ).wait()

    def got(slot, nx):
        return [
            [rbuf[slot, d, x : x + 1, :] for x in range(nx)] if d in (2, 3)
            else rbuf[slot, d, 0:8, :]
            for d in range(6)
        ]

    lane_base = (me[2] % 4) * 32

    def gather_copy(use, d):
        return pltpu.make_async_remote_copy(
            src_ref=gsend.at[use],
            dst_ref=gbuf.at[use, linear],
            send_sem=gssem.at[use],
            recv_sem=grsem.at[use],
            device_id=coords(d),
            device_id_type=MESH,
        )

    def gather_start(use, v):
        s = iota((8, 128), 0)
        straight = (s % 2) == (s // 4)
        packed = jnp.zeros((8, 128), F32)
        for x in range(4):
            both = jnp.where(straight, v[x], pltpu.roll(v[x], 4, 0))
            packed = jnp.where(s // 2 == x, both, packed)
        pick = (iota((128, 128), 0) == 4 * (iota((128, 128), 1) - lane_base)).astype(F32)
        packed = jnp.dot(packed, pick, precision=HIGHEST, preferred_element_type=F32)
        gsend[use] = packed
        gbuf[use, linear] = packed

        @pl.loop(1, count)
        def _(d):
            gather_copy(use, d).start()

    def gather_wait(use):
        whole = gbuf.at[use, pl.ds(0, count - 1)]
        pltpu.make_async_copy(whole, whole, gssem.at[use]).wait()
        pltpu.make_async_copy(whole, whole, grsem.at[use]).wait()
        rows = []
        for i in range(n_xy):
            parts = []
            for first in range(0, sz, 4):
                part = gbuf[use, i * sz + first]
                for j in range(first + 1, min(first + 4, sz)):
                    part = part + gbuf[use, i * sz + j]
                parts.append(part)
            rows.append(parts[0] if len(parts) == 1 else jnp.concatenate(parts, axis=1))
        return jnp.stack(rows)

    def set_up(c_ref, k, faces, halo, w):
        nx = k.shape[0]
        beside = rolled(k, w)
        shape = k.shape
        p, s, l = iota(shape, 0), iota(shape, 1), iota(shape, 2)
        masks = [p < 1, p >= nx - 1, s < w, s >= 8 - w, l < w, l >= 128 - w]
        total = jnp.zeros(shape, F32)
        for d in range(6):
            if d in (2, 3):
                far = spread_y([jnp.where(edge[d], a, b) for a, b in zip(faces[d], halo[d])])
            else:
                far = jnp.where(edge[d], faces[d], halo[d])
                far = spread_z(far, nx) if d >= 4 else jnp.broadcast_to(far[None], shape)
            c = float(w) * (0.5 * (k + jnp.where(masks[d], far, beside[d])))
            c_ref[d] = c
            total = total + c
        c_ref[6] = total
        c_ref[7] = 0.8 / total

    k0 = k_ref[...]
    k0_faces = own_faces(k0)
    send(0, k0_faces, 16)
    k1 = restrict(k0, 1) * 0.125
    k1_faces = own_faces(k1)
    send(1, k1_faces, 8)
    k2 = restrict(k1, 2) * 0.125
    gather_start(0, k2)

    receive(0, 16)
    set_up(c0, k0, k0_faces, got(0, 16), 1)
    receive(1, 8)
    set_up(c1, k1, k1_faces, got(1, 8), 2)

    phase = [0]

    def residual(c_ref, u, b, w, beside_wait=None):
        nx = u.shape[0]
        slot = 2 + phase[0] % 2
        phase[0] += 1
        send(slot, own_faces(u), nx)
        inner = rolled(u, w)
        r = b - c_ref[6] * u
        for d in range(6):
            r = r + c_ref[d] * inner[d]
        if beside_wait is not None:
            beside_wait()
        receive(slot, nx)
        halo = got(slot, nx)
        s, l = iota(u.shape, 1), iota(u.shape, 2)
        r = r + jnp.where(s < w, c_ref[2] * spread_y(halo[2]), 0.0)
        r = r + jnp.where(s >= 8 - w, c_ref[3] * spread_y(halo[3]), 0.0)
        r = r + jnp.where(l < w, c_ref[4] * spread_z(halo[4], nx), 0.0)
        r = r + jnp.where(l >= 128 - w, c_ref[5] * spread_z(halo[5], nx), 0.0)
        low = r[0] + c_ref[0, 0] * halo[0]
        high = r[nx - 1] + c_ref[1, nx - 1] * halo[1]
        return jnp.concatenate([low[None], r[1:-1], high[None]], axis=0)

    def sweep(c_ref, u, b, w, beside_wait=None):
        return u + c_ref[7] * residual(c_ref, u, b, w, beside_wait)

    def coarse_residual(v, b):
        beside = coarse_shifts(v, sx, sy, False)
        r = b - c2[6] * v
        for d in range(6):
            r = r + c2[d] * beside[d]
        return r

    def coarse_sweep(v, b):
        return v + c2[7] * coarse_residual(v, b)

    def coarse_set_up():
        k = gather_wait(0)
        beside = coarse_shifts(k, sx, sy, True)
        total = jnp.zeros_like(k)
        faces = []
        for d in range(6):
            c = 4.0 * (0.5 * (k + beside[d]))
            c2[d] = c
            faces.append(c)
            total = total + c
        c2[6] = total
        c2[7] = 0.8 / total
        s, l = iota(k.shape, 1), iota(k.shape, 2)
        outer = [s < 2, s >= 6, s % 2 == 0, s % 2 == 1, l % 32 == 0, l % 32 == 31]
        outward = [
            jnp.sum(jnp.where(m, c, 0.0), axis=1, keepdims=True) for m, c in zip(outer, faces)
        ]
        block = iota((1, lz), 1) // 32

        def owners(i, j, shift):
            row = jnp.full((1, lz), -1, jnp.int32)
            if not (0 <= i < sx and 0 <= j < sy):
                return row
            for z in range(sz):
                if 0 <= z + shift < sz:
                    row = jnp.where(block == z, owner_ref[i, j, z + shift], row)
            return row

        label = iota((GROUPS, lz), 0)
        system = jnp.zeros((GROUPS, GROUPS), F32)
        for i in range(sx):
            for j in range(sy):
                at = i * sy + j
                mine = owners(i, j, 0) == label
                member = jnp.where(mine, 1.0, 0.0)
                member_ref[at] = member
                out = [o[at] for o in outward]
                terms = jnp.where(mine, out[0] + out[1] + out[2] + out[3] + out[4] + out[5], 0.0)
                near = [(i - 1, j, 0), (i + 1, j, 0), (i, j - 1, 0), (i, j + 1, 0),
                        (i, j, -1), (i, j, 1)]
                for d in range(6):
                    terms = terms - jnp.where(owners(*near[d]) == label, out[d], 0.0)
                system = system + lax.dot_general(
                    member, terms, (((1,), (1,)), ((), ())), precision=HIGHEST,
                    preferred_element_type=F32)
        matrix_ref[...] = system

    def eliminate(first, last):
        rows, columns = iota((GROUPS, GROUPS), 0), iota((GROUPS, GROUPS), 1)
        a = matrix_ref[...]
        for step in range(first, last):
            at_row, at_column = rows == step, columns == step
            over = 1.0 / jnp.broadcast_to(a[step : step + 1, step : step + 1], (1, GROUPS))
            row = a[step : step + 1, :] * over
            column = jnp.broadcast_to(a[:, step : step + 1], (GROUPS, GROUPS))
            swept = jnp.where(at_column, column * over, a - column * row)
            a = jnp.where(at_row, jnp.where(at_column, -over, row), swept)
        matrix_ref[...] = a

    diagonal = iota((GROUPS, GROUPS), 0) == iota((GROUPS, GROUPS), 1)

    def coarse_solve(b, inverse):
        v = c2[7] * b
        for _ in range(SWEEPS - 1):
            v = coarse_sweep(v, b)
        sums = jnp.sum(coarse_residual(v, b), axis=1, keepdims=True)
        grouped = jnp.zeros((GROUPS, lz), F32)
        for i in range(n_xy):
            grouped = grouped + member_ref[i] * sums[i]
        rc = jnp.sum(grouped, axis=1, keepdims=True)
        xc = jnp.sum(inverse * rc, axis=0, keepdims=True)
        xc = jnp.sum(jnp.where(diagonal, xc, 0.0), axis=1, keepdims=True)
        lifted = jnp.stack([
            jnp.sum(member_ref[i] * xc, axis=0, keepdims=True) for i in range(n_xy)
        ])
        v = v + lifted
        for _ in range(SWEEPS):
            v = coarse_sweep(v, b)
        for first in range(lz // 128):
            wide_ref[:, first] = v[:, :, first * 128 : first * 128 + 128]
        mine = wide_ref[my_xy, me[2] // 4]
        put = (iota((128, 128), 0) == lane_base + iota((128, 128), 1) // 4).astype(F32)
        mine = jnp.dot(mine, put, precision=HIGHEST, preferred_element_type=F32)
        low = iota((8, 128), 0) < 4
        return jnp.stack([
            jnp.where(low, mine[2 * x : 2 * x + 1], mine[2 * x + 1 : 2 * x + 2])
            for x in range(4)
        ])

    def part(first, last):
        return lambda: eliminate(first, last)

    source = source_ref[...]
    u = None
    for cycle in range(CYCLES):
        first = cycle == 0
        u = c0[7] * source if first else sweep(c0, u, source, 1)
        u = sweep(c0, u, source, 1, coarse_set_up if first else None)
        b1 = restrict(residual(c0, u, source, 1, part(0, 4) if first else None), 1)
        u1 = c1[7] * b1
        u1 = sweep(c1, u1, b1, 2, part(4, 8) if first else None)
        b2 = restrict(residual(c1, u1, b1, 2, part(8, 12) if first else None), 2)
        gather_start(1 + cycle, b2)
        if first:
            eliminate(12, 16)
        u1 = u1 + prolong(coarse_solve(gather_wait(1 + cycle), -matrix_ref[...]))
        for _ in range(SWEEPS):
            u1 = sweep(c1, u1, b1, 2)
        u = u + prolong(u1)
        for _ in range(SWEEPS):
            u = sweep(c0, u, source, 1)
    sol_ref[...] = u
    res_ref[...] = residual(c0, u, source, 1)


def solution(mesh):
    sizes = tuple(mesh.shape[a] for a in AXES)
    sx, sy, sz = sizes
    count, n_xy, lz = sx * sy * sz, sx * sy, 32 * sz

    def on_device(source, conductivity, block_owner):
        vmem = pl.BlockSpec(memory_space=pltpu.VMEM)
        return pl.pallas_call(
            functools.partial(kernel, sizes),
            out_shape=[jax.ShapeDtypeStruct(source.shape, F32)] * 2,
            in_specs=[vmem, vmem, pl.BlockSpec(memory_space=pltpu.SMEM)],
            out_specs=[vmem, vmem],
            scratch_shapes=[
                pltpu.VMEM((4, 6, 16, 128), F32),
                pltpu.VMEM((4, 6, 16, 128), F32),
                pltpu.VMEM((3, 8, 128), F32),
                pltpu.VMEM((3, count, 8, 128), F32),
                pltpu.VMEM((8, 16, 8, 128), F32),
                pltpu.VMEM((8, 8, 8, 128), F32),
                pltpu.VMEM((8, n_xy, 8, lz), F32),
                pltpu.VMEM((n_xy, GROUPS, lz), F32),
                pltpu.VMEM((n_xy, lz // 128, 8, 128), F32),
                pltpu.VMEM((GROUPS, GROUPS), F32),
                pltpu.SemaphoreType.DMA((4, 6)),
                pltpu.SemaphoreType.DMA((4, 6)),
                pltpu.SemaphoreType.DMA((3,)),
                pltpu.SemaphoreType.DMA((3,)),
            ],
            compiler_params=pltpu.CompilerParams(
                collective_id=0, has_side_effects=True, vmem_limit_bytes=48 * 1024 * 1024
            ),
        )(source, conductivity, block_owner)

    spec = P(*AXES)
    return jax.shard_map(
        on_device, mesh=mesh, in_specs=(spec, spec, P()), out_specs=(spec, spec), check_vma=False
    )
```

```python
import functools

import jax
import jax.numpy as jnp
from jax import lax
from jax.experimental import pallas as pl
from jax.experimental.pallas import tpu as pltpu
from jax.sharding import PartitionSpec as P

GROUPS = 16
SWEEPS = 2
CYCLES = 2
F32 = jnp.float32
MESH = pl.DeviceIdType.MESH
HIGHEST = lax.Precision.HIGHEST
AXES = ("gx", "gy", "gz")


def iota(shape, dim):
    return lax.broadcasted_iota(jnp.int32, shape, dim)


def own_faces(u):
    nx = u.shape[0]
    lane, plane = iota(u.shape, 2), iota(u.shape, 0)
    z_low = jnp.sum(jnp.where(lane == plane, u[:, :, 0:1], 0.0), axis=0)
    z_high = jnp.sum(jnp.where(lane == plane, u[:, :, 127:128], 0.0), axis=0)
    y_low = [u[x, 0:1, :] for x in range(nx)]
    y_high = [u[x, 7:8, :] for x in range(nx)]
    return [u[0], u[nx - 1], y_low, y_high, z_low, z_high]


def spread_y(rows):
    return jnp.stack([jnp.broadcast_to(row, (8, 128)) for row in rows])


def spread_z(packed, nx):
    return jnp.stack([jnp.broadcast_to(packed[:, x : x + 1], (8, 128)) for x in range(nx)])


def rolled(u, w):
    s, l = iota(u.shape, 1), iota(u.shape, 2)
    gap = jnp.zeros((1, 8, 128), F32)
    return [
        jnp.concatenate([gap, u[:-1]], axis=0),
        jnp.concatenate([u[1:], gap], axis=0),
        jnp.where(s < w, 0.0, pltpu.roll(u, w, 1)),
        jnp.where(s >= 8 - w, 0.0, pltpu.roll(u, 8 - w, 1)),
        jnp.where(l < w, 0.0, pltpu.roll(u, w, 2)),
        jnp.where(l >= 128 - w, 0.0, pltpu.roll(u, 128 - w, 2)),
    ]


def pair_sum(v, w):
    s, l = iota(v.shape, 1), iota(v.shape, 2)
    v = v + jnp.where(s % (2 * w) < w, pltpu.roll(v, 8 - w, 1), pltpu.roll(v, w, 1))
    return v + jnp.where(l % (2 * w) < w, pltpu.roll(v, 128 - w, 2), pltpu.roll(v, w, 2))


def restrict(v, w):
    v = jnp.stack([v[2 * i] + v[2 * i + 1] for i in range(v.shape[0] // 2)])
    return pair_sum(v, w)


def prolong(v):
    return jnp.stack([v[i // 2] for i in range(2 * v.shape[0])])


def coarse_shifts(v, sx, sy, edge):
    s, l = iota(v.shape, 1), iota(v.shape, 2)
    lz = v.shape[2]
    own = v if edge else jnp.zeros_like(v)
    n = sx * sy

    def across_x(r, down):
        if sx == 1:
            return own
        if down:
            return jnp.concatenate([own[:sy], r[: n - sy]], axis=0)
        return jnp.concatenate([r[sy:], own[n - sy :]], axis=0)

    def across_y(r, down):
        parts = []
        for i in range(sx):
            a, b = i * sy, (i + 1) * sy
            inner = [r[a : b - 1]] if down else [r[a + 1 : b]]
            inner = inner if sy > 1 else []
            parts += ([own[a : a + 1]] + inner) if down else (inner + [own[b - 1 : b]])
        return jnp.concatenate(parts, axis=0)

    up2, down2 = pltpu.roll(v, 2, 1), pltpu.roll(v, 6, 1)
    up1, down1 = pltpu.roll(v, 1, 1), pltpu.roll(v, 7, 1)
    return [
        jnp.where(s < 2, across_x(up2, True), up2),
        jnp.where(s >= 6, across_x(down2, False), down2),
        jnp.where(s % 2 == 0, across_y(down1, True), up1),
        jnp.where(s % 2 == 1, across_y(up1, False), down1),
        jnp.where(l == 0, own, pltpu.roll(v, 1, 2)),
        jnp.where(l == lz - 1, own, pltpu.roll(v, lz - 1, 2)),
    ]


def kernel(sizes, source_ref, k_ref, owner_ref, sol_ref, res_ref,
           sbuf, rbuf, gsend, gbuf, c0, c1, c2, member_ref, wide_ref,
           ssem, rsem, gssem, grsem):
    sx, sy, sz = sizes
    count, n_xy, lz = sx * sy * sz, sx * sy, 32 * sz
    me = [lax.axis_index(a) for a in AXES]
    my_xy = me[0] * sy + me[1]
    linear = my_xy * sz + me[2]
    edge = [me[0] == 0, me[0] == sx - 1, me[1] == 0, me[1] == sy - 1, me[2] == 0, me[2] == sz - 1]

    rbuf[...] = jnp.zeros_like(rbuf)

    def coords(d):
        t = lax.rem(linear + d, count)
        return (t // (sy * sz), (t // sz) % sy, t % sz)

    def wrapped(a, step, size):
        t = me[a] + step
        return jnp.where(t >= size, t - size, t) if step else t

    def to_others(body):
        if count <= 64:
            tx = [wrapped(0, d, sx) for d in range(sx)]
            ty = [wrapped(1, d, sy) for d in range(sy)]
            tz = [wrapped(2, d, sz) for d in range(sz)]
            for i in range(sx):
                for j in range(sy):
                    for k in range(sz):
                        if i or j or k:
                            body((tx[i], ty[j], tz[k]))
        else:
            pl.loop(1, count)(lambda d: body(coords(d)))

    barrier = pltpu.get_barrier_semaphore()

    def greet(there):
        pl.semaphore_signal(barrier, inc=1, device_id=there, device_id_type=MESH)

    to_others(greet)
    pl.semaphore_wait(barrier, count - 1)

    def copy_of(slot, d, nx):
        axis, step = d // 2, 1 if d % 2 else -1
        there = [me[a] + step if a == axis else me[a] for a in range(3)]
        rows = nx if axis == 1 else 8
        return pltpu.make_async_remote_copy(
            src_ref=sbuf.at[slot, d, pl.ds(0, rows)],
            dst_ref=rbuf.at[slot, d ^ 1, pl.ds(0, rows)],
            send_sem=ssem.at[slot, d],
            recv_sem=rsem.at[slot, d ^ 1],
            device_id=tuple(there),
            device_id_type=MESH,
        )

    def send(slot, faces, nx):
        for d in (0, 1, 2, 3, 4, 5):
            if d in (2, 3):
                for x in range(nx):
                    sbuf[slot, d, x : x + 1, :] = faces[d][x]
            else:
                sbuf[slot, d, 0:8, :] = faces[d]

            @pl.when(jnp.logical_not(edge[d]))
            def _():
                copy_of(slot, d, nx).start()

    pending = []

    def receive(slot, nx):
        before = pending.pop() if pending else None
        pending.append((slot, nx))
        for d in range(6):
            @pl.when(jnp.logical_not(edge[d]))
            def _():
                if before:
                    copy_of(before[0], d, before[1]).wait_send()
                rows = nx if d // 2 == 1 else 8
                pltpu.make_async_copy(
                    rbuf.at[slot, d, pl.ds(0, rows)], rbuf.at[slot, d, pl.ds(0, rows)],
                    rsem.at[slot, d],
                ).wait()

    def got(slot, nx):
        return [
            [rbuf[slot, d, x : x + 1, :] for x in range(nx)] if d in (2, 3)
            else rbuf[slot, d, 0:8, :]
            for d in range(6)
        ]

    lane_base = (me[2] % 4) * 32

    def gather_copy(use, there):
        return pltpu.make_async_remote_copy(
            src_ref=gsend.at[use],
            dst_ref=gbuf.at[use, linear],
            send_sem=gssem.at[use],
            recv_sem=grsem.at[use],
            device_id=there,
            device_id_type=MESH,
        )

    def gather_start(use, v):
        s = iota((8, 128), 0)
        straight = (s % 2) == (s // 4)
        packed = jnp.zeros((8, 128), F32)
        for x in range(4):
            both = jnp.where(straight, v[x], pltpu.roll(v[x], 4, 0))
            packed = jnp.where(s // 2 == x, both, packed)
        pick = (iota((128, 128), 0) == 4 * (iota((128, 128), 1) % 32)).astype(F32)
        packed = jnp.dot(packed, pick, precision=HIGHEST, preferred_element_type=F32)
        part = iota((1, 128), 1) // 32
        for y in range(2):
            row = packed[y : y + 1]
            for x in range(1, 4):
                row = jnp.where(part == x, packed[2 * x + y : 2 * x + y + 1], row)
            gsend[use, y : y + 1, :] = row
            gbuf[use, linear, y : y + 1, :] = row
        to_others(lambda there: gather_copy(use, there).start())

    def gather_wait(use):
        whole = gbuf.at[use, pl.ds(0, count - 1)]
        pltpu.make_async_copy(whole, whole, grsem.at[use]).wait()
        turn = (iota((8, 128), 1) // 32 - iota((8, 128), 0) // 2 + 4) % 4
        rows = []
        for i in range(n_xy):
            parts = []
            for first in range(0, sz, 4):
                four = jnp.concatenate([gbuf[use, i * sz + first + j] for j in range(4)], axis=0)
                part = four
                for t in range(1, 4):
                    part = jnp.where(
                        turn == t, pltpu.roll(pltpu.roll(four, 32 * t, 1), 8 - 2 * t, 0), part)
                parts.append(part)
            rows.append(parts[0] if len(parts) == 1 else jnp.concatenate(parts, axis=1))
        return jnp.stack(rows)

    def set_up(c_ref, k, faces, halo, w):
        nx = k.shape[0]
        beside = rolled(k, w)
        shape = k.shape
        p, s, l = iota(shape, 0), iota(shape, 1), iota(shape, 2)
        masks = [p < 1, p >= nx - 1, s < w, s >= 8 - w, l < w, l >= 128 - w]
        total = jnp.zeros(shape, F32)
        for d in range(6):
            if d in (2, 3):
                far = spread_y([jnp.where(edge[d], a, b) for a, b in zip(faces[d], halo[d])])
            else:
                far = jnp.where(edge[d], faces[d], halo[d])
                far = spread_z(far, nx) if d >= 4 else jnp.broadcast_to(far[None], shape)
            c = float(w) * (0.5 * (k + jnp.where(masks[d], far, beside[d])))
            c_ref[d] = c
            total = total + c
        c_ref[6] = total
        c_ref[7] = 0.8 / total

    k0 = k_ref[...]
    k0_faces = own_faces(k0)
    send(0, k0_faces, 16)
    k1 = restrict(k0, 1) * 0.125
    k1_faces = own_faces(k1)
    send(1, k1_faces, 8)
    k2 = restrict(k1, 2) * 0.125
    gather_start(0, k2)

    receive(0, 16)
    set_up(c0, k0, k0_faces, got(0, 16), 1)
    receive(1, 8)
    set_up(c1, k1, k1_faces, got(1, 8), 2)

    phase = [0]

    def residual(c_ref, u, b, w, beside_wait=None):
        nx = u.shape[0]
        slot = 2 + phase[0] % 2
        phase[0] += 1
        send(slot, own_faces(u), nx)
        inner = rolled(u, w)
        r = b - c_ref[6] * u
        for d in range(6):
            r = r + c_ref[d] * inner[d]
        if beside_wait is not None:
            beside_wait()
        receive(slot, nx)
        halo = got(slot, nx)
        s, l = iota(u.shape, 1), iota(u.shape, 2)
        r = r + jnp.where(s < w, c_ref[2] * spread_y(halo[2]), 0.0)
        r = r + jnp.where(s >= 8 - w, c_ref[3] * spread_y(halo[3]), 0.0)
        r = r + jnp.where(l < w, c_ref[4] * spread_z(halo[4], nx), 0.0)
        r = r + jnp.where(l >= 128 - w, c_ref[5] * spread_z(halo[5], nx), 0.0)
        low = r[0] + c_ref[0, 0] * halo[0]
        high = r[nx - 1] + c_ref[1, nx - 1] * halo[1]
        return jnp.concatenate([low[None], r[1:-1], high[None]], axis=0)

    def sweep(c_ref, u, b, w):
        return u + c_ref[7] * residual(c_ref, u, b, w)

    def coarse_residual(v, b):
        beside = coarse_shifts(v, sx, sy, False)
        r = b - c2[6] * v
        for d in range(6):
            r = r + c2[d] * beside[d]
        return r

    def coarse_sweep(v, b):
        return v + c2[7] * coarse_residual(v, b)

    def coarse_set_up():
        k = gather_wait(0)
        beside = coarse_shifts(k, sx, sy, True)
        total = jnp.zeros_like(k)
        faces = []
        for d in range(6):
            c = 4.0 * (0.5 * (k + beside[d]))
            c2[d] = c
            faces.append(c)
            total = total + c
        c2[6] = total
        c2[7] = 0.8 / total
        s, l = iota(k.shape, 1), iota(k.shape, 2)
        outer = [s < 2, s >= 6, s % 2 == 0, s % 2 == 1, l % 32 == 0, l % 32 == 31]
        outward = [
            jnp.sum(jnp.where(m, c, 0.0), axis=1, keepdims=True) for m, c in zip(outer, faces)
        ]
        block = iota((1, lz), 1) // 32

        def owners(i, j, shift):
            row = jnp.full((1, lz), -1, jnp.int32)
            if not (0 <= i < sx and 0 <= j < sy):
                return row
            for z in range(sz):
                if 0 <= z + shift < sz:
                    row = jnp.where(block == z, owner_ref[i, j, z + shift], row)
            return row

        label = iota((GROUPS, lz), 0)
        system = jnp.zeros((GROUPS, GROUPS), F32)
        for i in range(sx):
            for j in range(sy):
                at = i * sy + j
                mine = owners(i, j, 0) == label
                member = jnp.where(mine, 1.0, 0.0)
                member_ref[at] = member
                out = [o[at] for o in outward]
                terms = jnp.where(mine, out[0] + out[1] + out[2] + out[3] + out[4] + out[5], 0.0)
                near = [(i - 1, j, 0), (i + 1, j, 0), (i, j - 1, 0), (i, j + 1, 0),
                        (i, j, -1), (i, j, 1)]
                for d in range(6):
                    terms = terms - jnp.where(owners(*near[d]) == label, out[d], 0.0)
                system = system + lax.dot_general(
                    member, terms, (((1,), (1,)), ((), ())), precision=HIGHEST,
                    preferred_element_type=F32)
        rows, columns = iota((GROUPS, GROUPS), 0), iota((GROUPS, GROUPS), 1)

        def eliminate(step, a):
            at_row, at_column = rows == step, columns == step
            row = jnp.sum(jnp.where(at_row, a, 0.0), axis=0, keepdims=True)
            column = jnp.sum(jnp.where(at_column, a, 0.0), axis=1, keepdims=True)
            pivot = jnp.sum(jnp.where(at_column, row, 0.0), axis=1, keepdims=True)
            over = 1.0 / pivot[0:1]
            swept = a - column * (row * over)
            swept = jnp.where(at_row, row * over, swept)
            swept = jnp.where(at_column, column * over, swept)
            return jnp.where(at_row & at_column, -over, swept)

        return -lax.fori_loop(0, GROUPS, eliminate, system)

    diagonal = iota((GROUPS, GROUPS), 0) == iota((GROUPS, GROUPS), 1)

    def coarse_solve(b, inverse):
        v = c2[7] * b
        for _ in range(SWEEPS - 1):
            v = coarse_sweep(v, b)
        sums = jnp.sum(coarse_residual(v, b), axis=1, keepdims=True)
        grouped = jnp.zeros((GROUPS, lz), F32)
        for i in range(n_xy):
            grouped = grouped + member_ref[i] * sums[i]
        rc = jnp.sum(grouped, axis=1, keepdims=True)
        xc = jnp.sum(inverse * rc, axis=0, keepdims=True)
        xc = jnp.sum(jnp.where(diagonal, xc, 0.0), axis=1, keepdims=True)
        lifted = jnp.stack([
            jnp.sum(member_ref[i] * xc, axis=0, keepdims=True) for i in range(n_xy)
        ])
        v = v + lifted
        for _ in range(SWEEPS):
            v = coarse_sweep(v, b)
        for first in range(lz // 128):
            wide_ref[:, first] = v[:, :, first * 128 : first * 128 + 128]
        mine = wide_ref[my_xy, me[2] // 4]
        put = (iota((128, 128), 0) == lane_base + iota((128, 128), 1) // 4).astype(F32)
        mine = jnp.dot(mine, put, precision=HIGHEST, preferred_element_type=F32)
        low = iota((8, 128), 0) < 4
        return jnp.stack([
            jnp.where(low, mine[2 * x : 2 * x + 1], mine[2 * x + 1 : 2 * x + 2])
            for x in range(4)
        ])

    source = source_ref[...]
    inverse = None
    u = None
    for cycle in range(CYCLES):
        if cycle == 0:
            u = c0[7] * source
        else:
            u = sweep(c0, u, source, 1)
        for _ in range(SWEEPS - 1):
            u = sweep(c0, u, source, 1)
        b1 = restrict(residual(c0, u, source, 1), 1)
        u1 = c1[7] * b1
        for _ in range(SWEEPS - 1):
            u1 = sweep(c1, u1, b1, 2)
        b2 = restrict(residual(c1, u1, b1, 2), 2)
        gather_start(1 + cycle, b2)
        if cycle == 0:
            inverse = coarse_set_up()
        u1 = u1 + prolong(coarse_solve(gather_wait(1 + cycle), inverse))
        for _ in range(SWEEPS):
            u1 = sweep(c1, u1, b1, 2)
        u = u + prolong(u1)
        for _ in range(SWEEPS):
            u = sweep(c0, u, source, 1)
    sol_ref[...] = u
    res_ref[...] = residual(c0, u, source, 1)
    for slot, nx in pending:
        for d in range(6):
            @pl.when(jnp.logical_not(edge[d]))
            def _():
                copy_of(slot, d, nx).wait_send()
    for use in range(1 + CYCLES):
        whole = gbuf.at[use, pl.ds(0, count - 1)]
        pltpu.make_async_copy(whole, whole, gssem.at[use]).wait()


def solution(mesh):
    sizes = tuple(mesh.shape[a] for a in AXES)
    sx, sy, sz = sizes
    count, n_xy, lz = sx * sy * sz, sx * sy, 32 * sz

    def on_device(source, conductivity, block_owner):
        vmem = pl.BlockSpec(memory_space=pltpu.VMEM)
        return pl.pallas_call(
            functools.partial(kernel, sizes),
            out_shape=[jax.ShapeDtypeStruct(source.shape, F32)] * 2,
            in_specs=[vmem, vmem, pl.BlockSpec(memory_space=pltpu.SMEM)],
            out_specs=[vmem, vmem],
            scratch_shapes=[
                pltpu.VMEM((4, 6, 16, 128), F32),
                pltpu.VMEM((4, 6, 16, 128), F32),
                pltpu.VMEM((3, 2, 128), F32),
                pltpu.VMEM((3, count, 2, 128), F32),
                pltpu.VMEM((8, 16, 8, 128), F32),
                pltpu.VMEM((8, 8, 8, 128), F32),
                pltpu.VMEM((8, n_xy, 8, lz), F32),
                pltpu.VMEM((n_xy, GROUPS, lz), F32),
                pltpu.VMEM((n_xy, lz // 128, 8, 128), F32),
                pltpu.SemaphoreType.DMA((4, 6)),
                pltpu.SemaphoreType.DMA((4, 6)),
                pltpu.SemaphoreType.DMA((3,)),
                pltpu.SemaphoreType.DMA((3,)),
            ],
            compiler_params=pltpu.CompilerParams(
                collective_id=0, has_side_effects=True, vmem_limit_bytes=48 * 1024 * 1024
            ),
        )(source, conductivity, block_owner)

    spec = P(*AXES)
    return jax.shard_map(
        on_device, mesh=mesh, in_specs=(spec, spec, P()), out_specs=(spec, spec), check_vma=False
    )
```

```python
import functools

import jax
import jax.numpy as jnp
from jax import lax
from jax.experimental import pallas as pl
from jax.experimental.pallas import tpu as pltpu
from jax.sharding import PartitionSpec as P

GROUPS = 16
SWEEPS = 2
CYCLES = 2
F32 = jnp.float32
MESH = pl.DeviceIdType.MESH
HIGHEST = lax.Precision.HIGHEST
AXES = ("gx", "gy", "gz")


def iota(shape, dim):
    return lax.broadcasted_iota(jnp.int32, shape, dim)


def own_faces(u):
    nx = u.shape[0]
    lane, plane = iota(u.shape, 2), iota(u.shape, 0)
    z_low = jnp.sum(jnp.where(lane == plane, u[:, :, 0:1], 0.0), axis=0)
    z_high = jnp.sum(jnp.where(lane == plane, u[:, :, 127:128], 0.0), axis=0)
    y_low = [u[x, 0:1, :] for x in range(nx)]
    y_high = [u[x, 7:8, :] for x in range(nx)]
    return [u[0], u[nx - 1], y_low, y_high, z_low, z_high]


def spread_y(rows):
    return jnp.stack([jnp.broadcast_to(row, (8, 128)) for row in rows])


def spread_z(packed, nx):
    return jnp.stack([jnp.broadcast_to(packed[:, x : x + 1], (8, 128)) for x in range(nx)])


def rolled(u, w):
    s, l = iota(u.shape, 1), iota(u.shape, 2)
    gap = jnp.zeros((1, 8, 128), F32)
    return [
        jnp.concatenate([gap, u[:-1]], axis=0),
        jnp.concatenate([u[1:], gap], axis=0),
        jnp.where(s < w, 0.0, pltpu.roll(u, w, 1)),
        jnp.where(s >= 8 - w, 0.0, pltpu.roll(u, 8 - w, 1)),
        jnp.where(l < w, 0.0, pltpu.roll(u, w, 2)),
        jnp.where(l >= 128 - w, 0.0, pltpu.roll(u, 128 - w, 2)),
    ]


def pair_sum(v, w):
    s, l = iota(v.shape, 1), iota(v.shape, 2)
    v = v + jnp.where(s % (2 * w) < w, pltpu.roll(v, 8 - w, 1), pltpu.roll(v, w, 1))
    return v + jnp.where(l % (2 * w) < w, pltpu.roll(v, 128 - w, 2), pltpu.roll(v, w, 2))


def restrict(v, w):
    v = jnp.stack([v[2 * i] + v[2 * i + 1] for i in range(v.shape[0] // 2)])
    return pair_sum(v, w)


def prolong(v):
    return jnp.stack([v[i // 2] for i in range(2 * v.shape[0])])


def coarse_shifts(v, sx, sy, edge):
    s, l = iota(v.shape, 1), iota(v.shape, 2)
    lz = v.shape[2]
    own = v if edge else jnp.zeros_like(v)
    n = sx * sy

    def across_x(r, down):
        if sx == 1:
            return own
        if down:
            return jnp.concatenate([own[:sy], r[: n - sy]], axis=0)
        return jnp.concatenate([r[sy:], own[n - sy :]], axis=0)

    def across_y(r, down):
        parts = []
        for i in range(sx):
            a, b = i * sy, (i + 1) * sy
            inner = [r[a : b - 1]] if down else [r[a + 1 : b]]
            inner = inner if sy > 1 else []
            parts += ([own[a : a + 1]] + inner) if down else (inner + [own[b - 1 : b]])
        return jnp.concatenate(parts, axis=0)

    up2, down2 = pltpu.roll(v, 2, 1), pltpu.roll(v, 6, 1)
    up1, down1 = pltpu.roll(v, 1, 1), pltpu.roll(v, 7, 1)
    return [
        jnp.where(s < 2, across_x(up2, True), up2),
        jnp.where(s >= 6, across_x(down2, False), down2),
        jnp.where(s % 2 == 0, across_y(down1, True), up1),
        jnp.where(s % 2 == 1, across_y(up1, False), down1),
        jnp.where(l == 0, own, pltpu.roll(v, 1, 2)),
        jnp.where(l == lz - 1, own, pltpu.roll(v, lz - 1, 2)),
    ]


def kernel(sizes, source_ref, k_ref, owner_ref, sol_ref, res_ref,
           sbuf, rbuf, gsend, gbuf, c0, c1, c2, member_ref, wide_ref,
           ssem, rsem, gssem, grsem):
    sx, sy, sz = sizes
    count, n_xy, lz = sx * sy * sz, sx * sy, 32 * sz
    me = [lax.axis_index(a) for a in AXES]
    my_xy = me[0] * sy + me[1]
    linear = my_xy * sz + me[2]
    edge = [me[0] == 0, me[0] == sx - 1, me[1] == 0, me[1] == sy - 1, me[2] == 0, me[2] == sz - 1]

    rbuf[...] = jnp.zeros_like(rbuf)

    def coords(d):
        t = lax.rem(linear + d, count)
        return (t // (sy * sz), (t // sz) % sy, t % sz)

    def wrapped(a, step, size):
        t = me[a] + step
        return jnp.where(t >= size, t - size, t) if step else t

    def to_others(body):
        if count <= 64:
            tx = [wrapped(0, d, sx) for d in range(sx)]
            ty = [wrapped(1, d, sy) for d in range(sy)]
            tz = [wrapped(2, d, sz) for d in range(sz)]
            for i in range(sx):
                for j in range(sy):
                    for k in range(sz):
                        if i or j or k:
                            body((tx[i], ty[j], tz[k]))
        else:
            pl.loop(1, count)(lambda d: body(coords(d)))

    barrier = pltpu.get_barrier_semaphore()

    def greet(there):
        pl.semaphore_signal(barrier, inc=1, device_id=there, device_id_type=MESH)

    to_others(greet)
    pl.semaphore_wait(barrier, count - 1)

    def copy_of(slot, d, nx):
        axis, step = d // 2, 1 if d % 2 else -1
        there = [me[a] + step if a == axis else me[a] for a in range(3)]
        rows = nx if axis == 1 else 8
        return pltpu.make_async_remote_copy(
            src_ref=sbuf.at[slot, d, pl.ds(0, rows)],
            dst_ref=rbuf.at[slot, d ^ 1, pl.ds(0, rows)],
            send_sem=ssem.at[slot, d],
            recv_sem=rsem.at[slot, d ^ 1],
            device_id=tuple(there),
            device_id_type=MESH,
        )

    def send(slot, faces, nx):
        for d in (0, 1, 2, 3, 4, 5):
            if d in (2, 3):
                for x in range(nx):
                    sbuf[slot, d, x : x + 1, :] = faces[d][x]
            else:
                sbuf[slot, d, 0:8, :] = faces[d]

            @pl.when(jnp.logical_not(edge[d]))
            def _():
                copy_of(slot, d, nx).start()

    pending = []

    def receive(slot, nx):
        before = pending.pop() if pending else None
        pending.append((slot, nx))
        for d in range(6):
            @pl.when(jnp.logical_not(edge[d]))
            def _():
                if before:
                    copy_of(before[0], d, before[1]).wait_send()
                rows = nx if d // 2 == 1 else 8
                pltpu.make_async_copy(
                    rbuf.at[slot, d, pl.ds(0, rows)], rbuf.at[slot, d, pl.ds(0, rows)],
                    rsem.at[slot, d],
                ).wait()

    def got(slot, nx):
        return [
            [rbuf[slot, d, x : x + 1, :] for x in range(nx)] if d in (2, 3)
            else rbuf[slot, d, 0:8, :]
            for d in range(6)
        ]

    lane_base = (me[2] % 4) * 32

    def gather_copy(use, there):
        return pltpu.make_async_remote_copy(
            src_ref=gsend.at[use],
            dst_ref=gbuf.at[use, linear],
            send_sem=gssem.at[use],
            recv_sem=grsem.at[use],
            device_id=there,
            device_id_type=MESH,
        )

    def gather_start(use, v):
        s = iota((8, 128), 0)
        straight = (s % 2) == (s // 4)
        packed = jnp.zeros((8, 128), F32)
        for x in range(4):
            both = jnp.where(straight, v[x], pltpu.roll(v[x], 4, 0))
            packed = jnp.where(s // 2 == x, both, packed)
        pick = (iota((128, 128), 0) == 4 * (iota((128, 128), 1) % 32)).astype(F32)
        packed = jnp.dot(packed, pick, precision=HIGHEST, preferred_element_type=F32)
        part = iota((1, 128), 1) // 32
        for y in range(2):
            row = packed[y : y + 1]
            for x in range(1, 4):
                row = jnp.where(part == x, packed[2 * x + y : 2 * x + y + 1], row)
            gsend[use, y : y + 1, :] = row
            gbuf[use, linear, y : y + 1, :] = row
        to_others(lambda there: gather_copy(use, there).start())

    def gather_wait(use):
        whole = gbuf.at[use, pl.ds(0, count - 1)]
        pltpu.make_async_copy(whole, whole, grsem.at[use]).wait()
        turn = (iota((8, 128), 1) // 32 - iota((8, 128), 0) // 2 + 4) % 4
        rows = []
        for i in range(n_xy):
            parts = []
            for first in range(0, sz, 4):
                four = jnp.concatenate([gbuf[use, i * sz + first + j] for j in range(4)], axis=0)
                part = four
                for t in range(1, 4):
                    part = jnp.where(
                        turn == t, pltpu.roll(pltpu.roll(four, 32 * t, 1), 8 - 2 * t, 0), part)
                parts.append(part)
            rows.append(parts[0] if len(parts) == 1 else jnp.concatenate(parts, axis=1))
        return jnp.stack(rows)

    def set_up(c_ref, k, faces, halo, w):
        nx = k.shape[0]
        beside = rolled(k, w)
        shape = k.shape
        p, s, l = iota(shape, 0), iota(shape, 1), iota(shape, 2)
        masks = [p < 1, p >= nx - 1, s < w, s >= 8 - w, l < w, l >= 128 - w]
        total = jnp.zeros(shape, F32)
        for d in range(6):
            if d in (2, 3):
                far = spread_y([jnp.where(edge[d], a, b) for a, b in zip(faces[d], halo[d])])
            else:
                far = jnp.where(edge[d], faces[d], halo[d])
                far = spread_z(far, nx) if d >= 4 else jnp.broadcast_to(far[None], shape)
            c = float(w) * (0.5 * (k + jnp.where(masks[d], far, beside[d])))
            c_ref[d] = c
            total = total + c
        c_ref[6] = total
        c_ref[7] = 0.8 / total

    k0 = k_ref[...]
    k0_faces = own_faces(k0)
    send(0, k0_faces, 16)
    k1 = restrict(k0, 1) * 0.125
    k1_faces = own_faces(k1)
    send(1, k1_faces, 8)
    k2 = restrict(k1, 2) * 0.125
    gather_start(0, k2)

    receive(0, 16)
    set_up(c0, k0, k0_faces, got(0, 16), 1)
    receive(1, 8)
    set_up(c1, k1, k1_faces, got(1, 8), 2)

    phase = [0]

    def residual(c_ref, u, b, w, lift=None):
        nx = u.shape[0]
        if lift is None:
            phase[0] += 1
        slot = 2 + phase[0] % 2
        if lift is None:
            send(slot, own_faces(u), nx)
        inner = rolled(u, w)
        r = b - c_ref[6] * u
        for d in range(6):
            r = r + c_ref[d] * inner[d]
        if lift is None:
            receive(slot, nx)
        halo = got(slot, nx)
        s, l = iota(u.shape, 1), iota(u.shape, 2)
        r = r + jnp.where(s < w, c_ref[2] * spread_y(halo[2]), 0.0)
        r = r + jnp.where(s >= 8 - w, c_ref[3] * spread_y(halo[3]), 0.0)
        r = r + jnp.where(l < w, c_ref[4] * spread_z(halo[4], nx), 0.0)
        r = r + jnp.where(l >= 128 - w, c_ref[5] * spread_z(halo[5], nx), 0.0)
        if lift is not None:
            inside = [s < w, s >= 8 - w, l < w, l >= 128 - w]
            for d in range(2, 6):
                r = r + jnp.where(inside[d - 2], c_ref[d] * lift[d], 0.0)
            halo[0] = halo[0] + lift[0][0]
            halo[1] = halo[1] + lift[1][nx - 1]
        low = r[0] + c_ref[0, 0] * halo[0]
        high = r[nx - 1] + c_ref[1, nx - 1] * halo[1]
        return jnp.concatenate([low[None], r[1:-1], high[None]], axis=0)

    def sweep(c_ref, u, b, w, lift=None):
        return u + c_ref[7] * residual(c_ref, u, b, w, lift)

    def coarse_residual(v, b):
        beside = coarse_shifts(v, sx, sy, False)
        r = b - c2[6] * v
        for d in range(6):
            r = r + c2[d] * beside[d]
        return r

    def coarse_sweep(v, b):
        return v + c2[7] * coarse_residual(v, b)

    def coarse_set_up():
        k = gather_wait(0)
        beside = coarse_shifts(k, sx, sy, True)
        total = jnp.zeros_like(k)
        faces = []
        for d in range(6):
            c = 4.0 * (0.5 * (k + beside[d]))
            c2[d] = c
            faces.append(c)
            total = total + c
        c2[6] = total
        c2[7] = 0.8 / total
        s, l = iota(k.shape, 1), iota(k.shape, 2)
        outer = [s < 2, s >= 6, s % 2 == 0, s % 2 == 1, l % 32 == 0, l % 32 == 31]
        outward = [
            jnp.sum(jnp.where(m, c, 0.0), axis=1, keepdims=True) for m, c in zip(outer, faces)
        ]
        block = iota((1, lz), 1) // 32

        def owners(i, j, shift):
            row = jnp.full((1, lz), -1, jnp.int32)
            if not (0 <= i < sx and 0 <= j < sy):
                return row
            for z in range(sz):
                if 0 <= z + shift < sz:
                    row = jnp.where(block == z, owner_ref[i, j, z + shift], row)
            return row

        label = iota((GROUPS, lz), 0)
        system = jnp.zeros((GROUPS, GROUPS), F32)
        for i in range(sx):
            for j in range(sy):
                at = i * sy + j
                mine = owners(i, j, 0) == label
                member = jnp.where(mine, 1.0, 0.0)
                member_ref[at] = member
                out = [o[at] for o in outward]
                terms = jnp.where(mine, out[0] + out[1] + out[2] + out[3] + out[4] + out[5], 0.0)
                near = [(i - 1, j, 0), (i + 1, j, 0), (i, j - 1, 0), (i, j + 1, 0),
                        (i, j, -1), (i, j, 1)]
                for d in range(6):
                    terms = terms - jnp.where(owners(*near[d]) == label, out[d], 0.0)
                system = system + lax.dot_general(
                    member, terms, (((1,), (1,)), ((), ())), precision=HIGHEST,
                    preferred_element_type=F32)
        rows, columns = iota((GROUPS, GROUPS), 0), iota((GROUPS, GROUPS), 1)

        def eliminate(step, a):
            at_row, at_column = rows == step, columns == step
            row = jnp.sum(jnp.where(at_row, a, 0.0), axis=0, keepdims=True)
            column = jnp.sum(jnp.where(at_column, a, 0.0), axis=1, keepdims=True)
            pivot = jnp.sum(jnp.where(at_column, row, 0.0), axis=1, keepdims=True)
            over = 1.0 / pivot[0:1]
            swept = a - column * (row * over)
            swept = jnp.where(at_row, row * over, swept)
            swept = jnp.where(at_column, column * over, swept)
            return jnp.where(at_row & at_column, -over, swept)

        return -lax.fori_loop(0, GROUPS, eliminate, system)

    diagonal = iota((GROUPS, GROUPS), 0) == iota((GROUPS, GROUPS), 1)

    def coarse_solve(b, inverse):
        v = c2[7] * b
        for _ in range(SWEEPS - 1):
            v = coarse_sweep(v, b)
        sums = jnp.sum(coarse_residual(v, b), axis=1, keepdims=True)
        grouped = jnp.zeros((GROUPS, lz), F32)
        for i in range(n_xy):
            grouped = grouped + member_ref[i] * sums[i]
        rc = jnp.sum(grouped, axis=1, keepdims=True)
        xc = jnp.sum(inverse * rc, axis=0, keepdims=True)
        xc = jnp.sum(jnp.where(diagonal, xc, 0.0), axis=1, keepdims=True)
        lifted = jnp.stack([
            jnp.sum(member_ref[i] * xc, axis=0, keepdims=True) for i in range(n_xy)
        ])
        v = v + lifted
        for _ in range(SWEEPS):
            v = coarse_sweep(v, b)
        fields = [v] + coarse_shifts(v, sx, sy, False)
        for f in range(7):
            for first in range(lz // 128):
                wide_ref[f, :, first] = fields[f][:, :, first * 128 : first * 128 + 128]
        mine = jnp.concatenate([wide_ref[f, my_xy, me[2] // 4] for f in range(7)], axis=0)
        put = (iota((128, 128), 0) == lane_base + iota((128, 128), 1) // 4).astype(F32)
        mine = jnp.dot(mine, put, precision=HIGHEST, preferred_element_type=F32)
        low = iota((8, 128), 0) < 4

        def on_level_one(f):
            at = 8 * f
            return prolong(jnp.stack([
                jnp.where(low, mine[at + 2 * x : at + 2 * x + 1],
                          mine[at + 2 * x + 1 : at + 2 * x + 2])
                for x in range(4)
            ]))

        return on_level_one(0), [on_level_one(f) for f in range(1, 7)]

    source = source_ref[...]
    inverse = None
    u = None
    for cycle in range(CYCLES):
        if cycle == 0:
            u = c0[7] * source
        else:
            u = sweep(c0, u, source, 1)
        for _ in range(SWEEPS - 1):
            u = sweep(c0, u, source, 1)
        b1 = restrict(residual(c0, u, source, 1), 1)
        u1 = c1[7] * b1
        for _ in range(SWEEPS - 1):
            u1 = sweep(c1, u1, b1, 2)
        b2 = restrict(residual(c1, u1, b1, 2), 2)
        gather_start(1 + cycle, b2)
        if cycle == 0:
            inverse = coarse_set_up()
        correction, lift = coarse_solve(gather_wait(1 + cycle), inverse)
        u1 = sweep(c1, u1 + correction, b1, 2, lift)
        for _ in range(SWEEPS - 1):
            u1 = sweep(c1, u1, b1, 2)
        u = u + prolong(u1)
        for _ in range(SWEEPS):
            u = sweep(c0, u, source, 1)
    sol_ref[...] = u
    res_ref[...] = residual(c0, u, source, 1)
    for slot, nx in pending:
        for d in range(6):
            @pl.when(jnp.logical_not(edge[d]))
            def _():
                copy_of(slot, d, nx).wait_send()
    for use in range(1 + CYCLES):
        whole = gbuf.at[use, pl.ds(0, count - 1)]
        pltpu.make_async_copy(whole, whole, gssem.at[use]).wait()


def solution(mesh):
    sizes = tuple(mesh.shape[a] for a in AXES)
    sx, sy, sz = sizes
    count, n_xy, lz = sx * sy * sz, sx * sy, 32 * sz

    def on_device(source, conductivity, block_owner):
        vmem = pl.BlockSpec(memory_space=pltpu.VMEM)
        return pl.pallas_call(
            functools.partial(kernel, sizes),
            out_shape=[jax.ShapeDtypeStruct(source.shape, F32)] * 2,
            in_specs=[vmem, vmem, pl.BlockSpec(memory_space=pltpu.SMEM)],
            out_specs=[vmem, vmem],
            scratch_shapes=[
                pltpu.VMEM((4, 6, 16, 128), F32),
                pltpu.VMEM((4, 6, 16, 128), F32),
                pltpu.VMEM((3, 2, 128), F32),
                pltpu.VMEM((3, count, 2, 128), F32),
                pltpu.VMEM((8, 16, 8, 128), F32),
                pltpu.VMEM((8, 8, 8, 128), F32),
                pltpu.VMEM((8, n_xy, 8, lz), F32),
                pltpu.VMEM((n_xy, GROUPS, lz), F32),
                pltpu.VMEM((7, n_xy, lz // 128, 8, 128), F32),
                pltpu.SemaphoreType.DMA((4, 6)),
                pltpu.SemaphoreType.DMA((4, 6)),
                pltpu.SemaphoreType.DMA((3,)),
                pltpu.SemaphoreType.DMA((3,)),
            ],
            compiler_params=pltpu.CompilerParams(
                collective_id=0, has_side_effects=True, vmem_limit_bytes=48 * 1024 * 1024
            ),
        )(source, conductivity, block_owner)

    spec = P(*AXES)
    return jax.shard_map(
        on_device, mesh=mesh, in_specs=(spec, spec, P()), out_specs=(spec, spec), check_vma=False
    )
```

```python
import functools

import jax
import jax.numpy as jnp
from jax import lax
from jax.experimental import pallas as pl
from jax.experimental.pallas import tpu as pltpu
from jax.sharding import PartitionSpec as P

GROUPS = 16
SWEEPS = 2
CYCLES = 2
F32 = jnp.float32
MESH = pl.DeviceIdType.MESH
HIGHEST = lax.Precision.HIGHEST
AXES = ("gx", "gy", "gz")


def iota(shape, dim):
    return lax.broadcasted_iota(jnp.int32, shape, dim)


def own_faces(u):
    nx = u.shape[0]
    lane, plane = iota(u.shape, 2), iota(u.shape, 0)
    z_low = jnp.sum(jnp.where(lane == plane, u[:, :, 0:1], 0.0), axis=0)
    z_high = jnp.sum(jnp.where(lane == plane, u[:, :, 127:128], 0.0), axis=0)
    y_low = [u[x, 0:1, :] for x in range(nx)]
    y_high = [u[x, 7:8, :] for x in range(nx)]
    return [u[0], u[nx - 1], y_low, y_high, z_low, z_high]


def spread_y(rows):
    return jnp.stack([jnp.broadcast_to(row, (8, 128)) for row in rows])


def spread_z(packed, nx):
    return jnp.stack([jnp.broadcast_to(packed[:, x : x + 1], (8, 128)) for x in range(nx)])


def rolled(u, w):
    s, l = iota(u.shape, 1), iota(u.shape, 2)
    gap = jnp.zeros((1, 8, 128), F32)
    return [
        jnp.concatenate([gap, u[:-1]], axis=0),
        jnp.concatenate([u[1:], gap], axis=0),
        jnp.where(s < w, 0.0, pltpu.roll(u, w, 1)),
        jnp.where(s >= 8 - w, 0.0, pltpu.roll(u, 8 - w, 1)),
        jnp.where(l < w, 0.0, pltpu.roll(u, w, 2)),
        jnp.where(l >= 128 - w, 0.0, pltpu.roll(u, 128 - w, 2)),
    ]


def pair_sum(v, w):
    s, l = iota(v.shape, 1), iota(v.shape, 2)
    v = v + jnp.where(s % (2 * w) < w, pltpu.roll(v, 8 - w, 1), pltpu.roll(v, w, 1))
    return v + jnp.where(l % (2 * w) < w, pltpu.roll(v, 128 - w, 2), pltpu.roll(v, w, 2))


def restrict(v, w):
    v = jnp.stack([v[2 * i] + v[2 * i + 1] for i in range(v.shape[0] // 2)])
    return pair_sum(v, w)


def prolong(v):
    return jnp.stack([v[i // 2] for i in range(2 * v.shape[0])])


def coarse_shifts(v, sx, sy, edge):
    s, l = iota(v.shape, 1), iota(v.shape, 2)
    lz = v.shape[2]
    own = v if edge else jnp.zeros_like(v)
    n = sx * sy

    def across_x(r, down):
        if sx == 1:
            return own
        if down:
            return jnp.concatenate([own[:sy], r[: n - sy]], axis=0)
        return jnp.concatenate([r[sy:], own[n - sy :]], axis=0)

    def across_y(r, down):
        parts = []
        for i in range(sx):
            a, b = i * sy, (i + 1) * sy
            inner = [r[a : b - 1]] if down else [r[a + 1 : b]]
            inner = inner if sy > 1 else []
            parts += ([own[a : a + 1]] + inner) if down else (inner + [own[b - 1 : b]])
        return jnp.concatenate(parts, axis=0)

    up2, down2 = pltpu.roll(v, 2, 1), pltpu.roll(v, 6, 1)
    up1, down1 = pltpu.roll(v, 1, 1), pltpu.roll(v, 7, 1)
    return [
        jnp.where(s < 2, across_x(up2, True), up2),
        jnp.where(s >= 6, across_x(down2, False), down2),
        jnp.where(s % 2 == 0, across_y(down1, True), up1),
        jnp.where(s % 2 == 1, across_y(up1, False), down1),
        jnp.where(l == 0, own, pltpu.roll(v, 1, 2)),
        jnp.where(l == lz - 1, own, pltpu.roll(v, lz - 1, 2)),
    ]


def kernel(sizes, source_ref, k_ref, owner_ref, sol_ref, res_ref,
           sbuf, rbuf, gsend, gbuf, c0, c1, c2, member_ref, wide_ref,
           ssem, rsem, gssem, grsem):
    sx, sy, sz = sizes
    count, n_xy, lz = sx * sy * sz, sx * sy, 32 * sz
    me = [lax.axis_index(a) for a in AXES]
    my_xy = me[0] * sy + me[1]
    linear = my_xy * sz + me[2]
    edge = [me[0] == 0, me[0] == sx - 1, me[1] == 0, me[1] == sy - 1, me[2] == 0, me[2] == sz - 1]

    rbuf[...] = jnp.zeros_like(rbuf)

    def coords(d):
        t = lax.rem(linear + d, count)
        return (t // (sy * sz), (t // sz) % sy, t % sz)

    def wrapped(a, step, size):
        t = me[a] + step
        return jnp.where(t >= size, t - size, t) if step else t

    def to_others(body):
        if count <= 64:
            tx = [wrapped(0, d, sx) for d in range(sx)]
            ty = [wrapped(1, d, sy) for d in range(sy)]
            tz = [wrapped(2, d, sz) for d in range(sz)]
            for i in reversed(range(sx)):
                for j in reversed(range(sy)):
                    for k in reversed(range(sz)):
                        if i or j or k:
                            body((tx[i], ty[j], tz[k]))
        else:
            pl.loop(1, count)(lambda d: body(coords(d)))

    barrier = pltpu.get_barrier_semaphore()

    def greet(there):
        pl.semaphore_signal(barrier, inc=1, device_id=there, device_id_type=MESH)

    to_others(greet)
    pl.semaphore_wait(barrier, count - 1)

    def copy_of(slot, d, nx):
        axis, step = d // 2, 1 if d % 2 else -1
        there = [me[a] + step if a == axis else me[a] for a in range(3)]
        rows = nx if axis == 1 else 8
        return pltpu.make_async_remote_copy(
            src_ref=sbuf.at[slot, d, pl.ds(0, rows)],
            dst_ref=rbuf.at[slot, d ^ 1, pl.ds(0, rows)],
            send_sem=ssem.at[slot, d],
            recv_sem=rsem.at[slot, d ^ 1],
            device_id=tuple(there),
            device_id_type=MESH,
        )

    def send(slot, faces, nx):
        for d in (0, 1, 2, 3, 4, 5):
            if d in (2, 3):
                for x in range(nx):
                    sbuf[slot, d, x : x + 1, :] = faces[d][x]
            else:
                sbuf[slot, d, 0:8, :] = faces[d]

            @pl.when(jnp.logical_not(edge[d]))
            def _():
                copy_of(slot, d, nx).start()

    pending = []

    def receive(slot, nx):
        before = pending.pop() if pending else None
        pending.append((slot, nx))
        for d in range(6):
            @pl.when(jnp.logical_not(edge[d]))
            def _():
                if before:
                    copy_of(before[0], d, before[1]).wait_send()
                rows = nx if d // 2 == 1 else 8
                pltpu.make_async_copy(
                    rbuf.at[slot, d, pl.ds(0, rows)], rbuf.at[slot, d, pl.ds(0, rows)],
                    rsem.at[slot, d],
                ).wait()

    def got(slot, nx):
        return [
            [rbuf[slot, d, x : x + 1, :] for x in range(nx)] if d in (2, 3)
            else rbuf[slot, d, 0:8, :]
            for d in range(6)
        ]

    lane_base = (me[2] % 4) * 32

    def gather_copy(use, there):
        return pltpu.make_async_remote_copy(
            src_ref=gsend.at[use],
            dst_ref=gbuf.at[use, linear],
            send_sem=gssem.at[use],
            recv_sem=grsem.at[use],
            device_id=there,
            device_id_type=MESH,
        )

    def gather_start(use, v):
        s = iota((8, 128), 0)
        straight = (s % 2) == (s // 4)
        packed = jnp.zeros((8, 128), F32)
        for x in range(4):
            both = jnp.where(straight, v[x], pltpu.roll(v[x], 4, 0))
            packed = jnp.where(s // 2 == x, both, packed)
        pick = (iota((128, 128), 0) == 4 * (iota((128, 128), 1) % 32)).astype(F32)
        packed = jnp.dot(packed, pick, precision=HIGHEST, preferred_element_type=F32)
        part = iota((1, 128), 1) // 32
        for y in range(2):
            row = packed[y : y + 1]
            for x in range(1, 4):
                row = jnp.where(part == x, packed[2 * x + y : 2 * x + y + 1], row)
            gsend[use, y : y + 1, :] = row
            gbuf[use, linear, y : y + 1, :] = row
        to_others(lambda there: gather_copy(use, there).start())

    def gather_wait(use):
        whole = gbuf.at[use, pl.ds(0, count - 1)]
        pltpu.make_async_copy(whole, whole, grsem.at[use]).wait()
        turn = (iota((8, 128), 1) // 32 - iota((8, 128), 0) // 2 + 4) % 4
        rows = []
        for i in range(n_xy):
            parts = []
            for first in range(0, sz, 4):
                four = jnp.concatenate([gbuf[use, i * sz + first + j] for j in range(4)], axis=0)
                part = four
                for t in range(1, 4):
                    part = jnp.where(
                        turn == t, pltpu.roll(pltpu.roll(four, 32 * t, 1), 8 - 2 * t, 0), part)
                parts.append(part)
            rows.append(parts[0] if len(parts) == 1 else jnp.concatenate(parts, axis=1))
        return jnp.stack(rows)

    def set_up(c_ref, k, faces, halo, w):
        nx = k.shape[0]
        beside = rolled(k, w)
        shape = k.shape
        p, s, l = iota(shape, 0), iota(shape, 1), iota(shape, 2)
        masks = [p < 1, p >= nx - 1, s < w, s >= 8 - w, l < w, l >= 128 - w]
        total = jnp.zeros(shape, F32)
        for d in range(6):
            if d in (2, 3):
                far = spread_y([jnp.where(edge[d], a, b) for a, b in zip(faces[d], halo[d])])
            else:
                far = jnp.where(edge[d], faces[d], halo[d])
                far = spread_z(far, nx) if d >= 4 else jnp.broadcast_to(far[None], shape)
            c = float(w) * (0.5 * (k + jnp.where(masks[d], far, beside[d])))
            c_ref[d] = c
            total = total + c
        c_ref[6] = total
        c_ref[7] = 0.8 / total

    k0 = k_ref[...]
    k0_faces = own_faces(k0)
    send(0, k0_faces, 16)
    k1 = restrict(k0, 1) * 0.125
    k1_faces = own_faces(k1)
    send(1, k1_faces, 8)
    k2 = restrict(k1, 2) * 0.125
    gather_start(0, k2)

    receive(0, 16)
    set_up(c0, k0, k0_faces, got(0, 16), 1)
    receive(1, 8)
    set_up(c1, k1, k1_faces, got(1, 8), 2)

    phase = [0]

    def residual(c_ref, u, b, w, lift=None):
        nx = u.shape[0]
        if lift is None:
            phase[0] += 1
        slot = 2 + phase[0] % 2
        if lift is None:
            send(slot, own_faces(u), nx)
        inner = rolled(u, w)
        r = b - c_ref[6] * u
        for d in range(6):
            r = r + c_ref[d] * inner[d]
        if lift is None:
            receive(slot, nx)
        halo = got(slot, nx)
        s, l = iota(u.shape, 1), iota(u.shape, 2)
        r = r + jnp.where(s < w, c_ref[2] * spread_y(halo[2]), 0.0)
        r = r + jnp.where(s >= 8 - w, c_ref[3] * spread_y(halo[3]), 0.0)
        r = r + jnp.where(l < w, c_ref[4] * spread_z(halo[4], nx), 0.0)
        r = r + jnp.where(l >= 128 - w, c_ref[5] * spread_z(halo[5], nx), 0.0)
        if lift is not None:
            inside = [s < w, s >= 8 - w, l < w, l >= 128 - w]
            for d in range(2, 6):
                r = r + jnp.where(inside[d - 2], c_ref[d] * lift[d], 0.0)
            halo[0] = halo[0] + lift[0][0]
            halo[1] = halo[1] + lift[1][nx - 1]
        low = r[0] + c_ref[0, 0] * halo[0]
        high = r[nx - 1] + c_ref[1, nx - 1] * halo[1]
        return jnp.concatenate([low[None], r[1:-1], high[None]], axis=0)

    def sweep(c_ref, u, b, w, lift=None):
        return u + c_ref[7] * residual(c_ref, u, b, w, lift)

    def coarse_residual(v, b):
        beside = coarse_shifts(v, sx, sy, False)
        r = b - c2[6] * v
        for d in range(6):
            r = r + c2[d] * beside[d]
        return r

    def coarse_sweep(v, b):
        return v + c2[7] * coarse_residual(v, b)

    def coarse_set_up():
        k = gather_wait(0)
        beside = coarse_shifts(k, sx, sy, True)
        total = jnp.zeros_like(k)
        faces = []
        for d in range(6):
            c = 4.0 * (0.5 * (k + beside[d]))
            c2[d] = c
            faces.append(c)
            total = total + c
        c2[6] = total
        c2[7] = 0.8 / total
        s, l = iota(k.shape, 1), iota(k.shape, 2)
        outer = [s < 2, s >= 6, s % 2 == 0, s % 2 == 1, l % 32 == 0, l % 32 == 31]
        outward = [
            jnp.sum(jnp.where(m, c, 0.0), axis=1, keepdims=True) for m, c in zip(outer, faces)
        ]
        block = iota((1, lz), 1) // 32

        def owners(i, j, shift):
            row = jnp.full((1, lz), -1, jnp.int32)
            if not (0 <= i < sx and 0 <= j < sy):
                return row
            for z in range(sz):
                if 0 <= z + shift < sz:
                    row = jnp.where(block == z, owner_ref[i, j, z + shift], row)
            return row

        label = iota((GROUPS, lz), 0)
        system = jnp.zeros((GROUPS, GROUPS), F32)
        for i in range(sx):
            for j in range(sy):
                at = i * sy + j
                mine = owners(i, j, 0) == label
                member = jnp.where(mine, 1.0, 0.0)
                member_ref[at] = member
                out = [o[at] for o in outward]
                terms = jnp.where(mine, out[0] + out[1] + out[2] + out[3] + out[4] + out[5], 0.0)
                near = [(i - 1, j, 0), (i + 1, j, 0), (i, j - 1, 0), (i, j + 1, 0),
                        (i, j, -1), (i, j, 1)]
                for d in range(6):
                    terms = terms - jnp.where(owners(*near[d]) == label, out[d], 0.0)
                system = system + lax.dot_general(
                    member, terms, (((1,), (1,)), ((), ())), precision=HIGHEST,
                    preferred_element_type=F32)
        rows, columns = iota((GROUPS, GROUPS), 0), iota((GROUPS, GROUPS), 1)

        a = system
        for step in range(GROUPS):
            at_row, at_column = rows == step, columns == step
            over = 1.0 / jnp.broadcast_to(a[step : step + 1, step : step + 1], (1, GROUPS))
            row = a[step : step + 1, :] * over
            column = jnp.broadcast_to(a[:, step : step + 1], (GROUPS, GROUPS))
            swept = jnp.where(at_column, column * over, a - column * row)
            a = jnp.where(at_row, jnp.where(at_column, -over, row), swept)
        return -a

    diagonal = iota((GROUPS, GROUPS), 0) == iota((GROUPS, GROUPS), 1)

    def coarse_solve(b, inverse):
        v = c2[7] * b
        for _ in range(SWEEPS - 1):
            v = coarse_sweep(v, b)
        sums = jnp.sum(coarse_residual(v, b), axis=1, keepdims=True)
        grouped = jnp.zeros((GROUPS, lz), F32)
        for i in range(n_xy):
            grouped = grouped + member_ref[i] * sums[i]
        rc = jnp.sum(grouped, axis=1, keepdims=True)
        xc = jnp.sum(inverse * rc, axis=0, keepdims=True)
        xc = jnp.sum(jnp.where(diagonal, xc, 0.0), axis=1, keepdims=True)
        lifted = jnp.stack([
            jnp.sum(member_ref[i] * xc, axis=0, keepdims=True) for i in range(n_xy)
        ])
        v = v + lifted
        for _ in range(SWEEPS):
            v = coarse_sweep(v, b)
        fields = [v] + coarse_shifts(v, sx, sy, False)
        for f in range(7):
            for first in range(lz // 128):
                wide_ref[f, :, first] = fields[f][:, :, first * 128 : first * 128 + 128]
        mine = jnp.concatenate([wide_ref[f, my_xy, me[2] // 4] for f in range(7)], axis=0)
        put = (iota((128, 128), 0) == lane_base + iota((128, 128), 1) // 4).astype(F32)
        mine = jnp.dot(mine, put, precision=HIGHEST, preferred_element_type=F32)
        low = iota((8, 128), 0) < 4

        def on_level_one(f):
            at = 8 * f
            return prolong(jnp.stack([
                jnp.where(low, mine[at + 2 * x : at + 2 * x + 1],
                          mine[at + 2 * x + 1 : at + 2 * x + 2])
                for x in range(4)
            ]))

        return on_level_one(0), [on_level_one(f) for f in range(1, 7)]

    source = source_ref[...]
    inverse = None
    u = None
    for cycle in range(CYCLES):
        if cycle == 0:
            u = c0[7] * source
        else:
            u = sweep(c0, u, source, 1)
        for _ in range(SWEEPS - 1):
            u = sweep(c0, u, source, 1)
        b1 = restrict(residual(c0, u, source, 1), 1)
        u1 = c1[7] * b1
        for _ in range(SWEEPS - 1):
            u1 = sweep(c1, u1, b1, 2)
        b2 = restrict(residual(c1, u1, b1, 2), 2)
        gather_start(1 + cycle, b2)
        if cycle == 0:
            inverse = coarse_set_up()
        correction, lift = coarse_solve(gather_wait(1 + cycle), inverse)
        u1 = sweep(c1, u1 + correction, b1, 2, lift)
        for _ in range(SWEEPS - 1):
            u1 = sweep(c1, u1, b1, 2)
        u = u + prolong(u1)
        for _ in range(SWEEPS):
            u = sweep(c0, u, source, 1)
    sol_ref[...] = u
    res_ref[...] = residual(c0, u, source, 1)
    for slot, nx in pending:
        for d in range(6):
            @pl.when(jnp.logical_not(edge[d]))
            def _():
                copy_of(slot, d, nx).wait_send()
    for use in range(1 + CYCLES):
        whole = gbuf.at[use, pl.ds(0, count - 1)]
        pltpu.make_async_copy(whole, whole, gssem.at[use]).wait()


def solution(mesh):
    sizes = tuple(mesh.shape[a] for a in AXES)
    sx, sy, sz = sizes
    count, n_xy, lz = sx * sy * sz, sx * sy, 32 * sz

    def on_device(source, conductivity, block_owner):
        vmem = pl.BlockSpec(memory_space=pltpu.VMEM)
        return pl.pallas_call(
            functools.partial(kernel, sizes),
            out_shape=[jax.ShapeDtypeStruct(source.shape, F32)] * 2,
            in_specs=[vmem, vmem, pl.BlockSpec(memory_space=pltpu.SMEM)],
            out_specs=[vmem, vmem],
            scratch_shapes=[
                pltpu.VMEM((4, 6, 16, 128), F32),
                pltpu.VMEM((4, 6, 16, 128), F32),
                pltpu.VMEM((3, 2, 128), F32),
                pltpu.VMEM((3, count, 2, 128), F32),
                pltpu.VMEM((8, 16, 8, 128), F32),
                pltpu.VMEM((8, 8, 8, 128), F32),
                pltpu.VMEM((8, n_xy, 8, lz), F32),
                pltpu.VMEM((n_xy, GROUPS, lz), F32),
                pltpu.VMEM((7, n_xy, lz // 128, 8, 128), F32),
                pltpu.SemaphoreType.DMA((4, 6)),
                pltpu.SemaphoreType.DMA((4, 6)),
                pltpu.SemaphoreType.DMA((3,)),
                pltpu.SemaphoreType.DMA((3,)),
            ],
            compiler_params=pltpu.CompilerParams(
                collective_id=0, has_side_effects=True, vmem_limit_bytes=48 * 1024 * 1024
            ),
        )(source, conductivity, block_owner)

    spec = P(*AXES)
    return jax.shard_map(
        on_device, mesh=mesh, in_specs=(spec, spec, P()), out_specs=(spec, spec), check_vma=False
    )
```
